128 devices in a mesh: ctx: 32 (over x, y_lo, z), tp: 4 (over y_hi, core).
Axes of the slice: x: 4, y: 4 (y_hi: 2, y_lo: 2; y = y_hi * 2 + y_lo), z: 4, core: 2. Of those that a mesh axis runs over, the one named last changes fastest.
Arguments:
- projected: bfloat16 [3, 4096, 4096], P(None, 'tp', 'ctx'), may hold values from -6 to 6
- conv_weight: float32 [7, 3, 4096], P(None, None, 'tp'), may hold values from -2 to 2
- filters: float32 [4, 64, 4096], P('tp', 'ctx'), may hold values from -6 to 6
- skip_gain: float32 [4096], P('tp'), may hold values from -1 to 1
- out_weight: bfloat16 [4096, 4096], P('tp', 'ctx'), may hold values from -0.09375 to 0.09375
- cotangent: bfloat16 [4096, 4096], P('tp', 'ctx'), may hold values from -6 to 6
Outputs:
- block_out: bfloat16 [4096, 4096], P('tp', 'ctx')
- proj_grad: bfloat16 [3, 4096, 4096], P(None, 'tp', 'ctx')
- filter_grad: float32 [4, 64, 4096], P('tp', 'ctx')
The draws below stay inside these ranges and needn't reach their ends.
All inputs are finite; a program needn't handle non-finite values.
Results may differ from the reference program's by a relative error of at most 0.017.
Values may be sent and summed in bfloat16 or wider, within the bound.
A program may use at most 128 MiB of HBM per device.

```python
import math
import jax
import jax.numpy as jnp
from jax import lax

D = 4096
OUT = 4096
GROUP = 16
KERNEL = 7
GROUPS = 256
LENGTH = 4096
N_TP = 4


def draw_filters(key, part):
    key = jax.random.fold_in(key, 7)
    keys = jax.random.split(key, 6)
    heads = (N_TP, GROUPS // N_TP)
    shape = (N_TP, GROUPS // N_TP, LENGTH)
    times = jnp.arange(LENGTH).astype(jnp.float32)
    slow_share = 0.5
    lasting = jax.random.bernoulli(keys[0], slow_share, heads)
    quick = jnp.exp(jax.random.uniform(keys[1], heads, jnp.float32, math.log(30.0), math.log(50.0)))
    steady = jnp.exp(jax.random.uniform(keys[2], heads, jnp.float32, math.log(1.0 * LENGTH), math.log(8.0 * LENGTH)))
    decay = jnp.where(lasting, steady, quick)
    spots = jax.random.randint(keys[3], heads + (2,), 1, LENGTH).astype(jnp.float32)
    drops = jax.random.uniform(keys[4], heads + (2,), jnp.float32, 0.55, 0.8)
    envelope = jnp.exp(-times / decay[..., None])
    for which in range(2):
        envelope = envelope * jnp.where(times >= spots[..., which, None], drops[..., which, None], 1.0)
    energy = 0.5 * decay * (1.0 - jnp.exp(-2.0 * LENGTH / decay)) + 1.0
    noise = jax.random.truncated_normal(keys[5], -6.0, 6.0, shape, jnp.float32)
    return (noise * envelope / jnp.sqrt(energy)[..., None]).astype(jnp.float32)


def level_of(key, shape, shards, least, top_value):
    factor_of = 1.0
    for axis_at, blocks in shards:
        steps = jax.random.uniform(jax.random.fold_in(jax.random.fold_in(key, 6), axis_at), (blocks,), jnp.float32, least / len(shards), top_value / len(shards))
        factor_of = factor_of * jnp.repeat(jnp.exp(steps), shape[axis_at] // blocks).reshape((-1,) + (1,) * (len(shape) - 1 - axis_at))
    return factor_of


def gaussian(own_key, shape, spread, reach, shards=(), kind=jnp.bfloat16):
    level = level_of(own_key, shape, shards, -0.22, 0.18) if shards else 1.0
    array = jax.random.normal(own_key, shape, jnp.float32) * spread * level
    return jnp.minimum(jnp.maximum(array, -reach), reach).astype(kind)


def setup_inputs(seed: int = 0) -> dict:
    seeds = jax.random.split(jax.random.key(seed), 7)
    projected = gaussian(seeds[0], (3, D, LENGTH), 1.0, 6.0, ((1, 4), (2, 32)))
    conv_weight = gaussian(seeds[1], (KERNEL, 3, D), KERNEL ** -0.5, 2.0, ((2, 4),), jnp.float32)
    filters = draw_filters(jax.random.fold_in(seeds[6], 71), 0)
    skip_gain = jnp.clip(jax.random.uniform(seeds[3], (D,), jnp.float32, -1.0, 1.0) * level_of(seeds[3], (D,), ((0, 4),), -0.4, 0.0), -1.0, 1.0)
    out_weight = gaussian(seeds[4], (D, OUT), D ** -0.5, 0.09375, ((0, 4), (1, 32)))
    cotangent = gaussian(seeds[5], (OUT, LENGTH), 1.0, 6.0, ((0, 4), (1, 32)))
    return {"projected": projected, "conv_weight": conv_weight, "filters": filters, "skip_gain": skip_gain, "out_weight": out_weight, "cotangent": cotangent}


precise = lax.Precision.HIGHEST

def short_stream(stream, weights):
    values = stream.astype(jnp.float32)
    padded = jnp.pad(values, ((0, 0), (KERNEL - 1, 0)))
    summed = jnp.zeros(values.shape, jnp.float32)
    for offset in range(KERNEL):
        begin_at = KERNEL - 1 - offset
        summed = summed + weights[offset][:, None] * padded[:, begin_at:begin_at + LENGTH]
    return summed.astype(jnp.bfloat16)

def short_stream_grad(upstream, weights):
    values = upstream.astype(jnp.float32)
    padded = jnp.pad(values, ((0, 0), (0, KERNEL - 1)))
    summed = jnp.zeros(values.shape, jnp.float32)
    for offset in range(KERNEL):
        summed = summed + weights[offset][:, None] * padded[:, offset:offset + LENGTH]
    return summed.astype(jnp.bfloat16)

def spectral_block(inputs):
    mix_blk, dlong_blk, taps, skip_rows = inputs
    padded_len = 2 * LENGTH
    mix_vals = mix_blk.astype(jnp.float32)
    dlong_vals = dlong_blk.astype(jnp.float32)
    mix_f = jnp.fft.rfft(mix_vals, n=padded_len)
    tap_f = jnp.fft.rfft(taps.astype(jnp.float32), n=padded_len)[:, None, :]
    dlong_f = jnp.fft.rfft(dlong_vals, n=padded_len)
    longmix = jnp.fft.irfft(mix_f * tap_f, n=padded_len)[..., :LENGTH] + skip_rows[..., None] * mix_vals
    dmix_input = jnp.fft.irfft(dlong_f * jnp.conj(tap_f), n=padded_len)[..., :LENGTH] + skip_rows[..., None] * dlong_vals
    cross = lax.optimization_barrier(jnp.sum(dlong_f * jnp.conj(mix_f), axis=1))
    filter_grad = jnp.fft.irfft(cross, n=padded_len)[..., :LENGTH] * (1.0 / math.sqrt(GROUP * LENGTH))
    return (longmix.astype(jnp.bfloat16), dmix_input.astype(jnp.bfloat16), filter_grad)

def reference(projected, conv_weight, filters, skip_gain, out_weight, cotangent):
    short_out = jnp.stack([short_stream(projected[stream_no], conv_weight[:, stream_no]) for stream_no in range(3)])
    mix_input = (short_out[1].astype(jnp.float32) * short_out[2].astype(jnp.float32)).astype(jnp.bfloat16)
    weight_vals = out_weight.astype(jnp.float32)
    dgated = jnp.dot(weight_vals, cotangent.astype(jnp.float32), precision=precise).astype(jnp.bfloat16)
    dlongmix = (dgated.astype(jnp.float32) * short_out[0].astype(jnp.float32)).astype(jnp.bfloat16)
    blocks = GROUPS // 8
    mix_b = mix_input.reshape(blocks, 8, GROUP, LENGTH)
    dlong_b = dlongmix.reshape(blocks, 8, GROUP, LENGTH)
    taps_b = filters.reshape(blocks, 8, LENGTH)
    skip_b = skip_gain.reshape(blocks, 8, GROUP)
    longmix, dmix_input, filter_grad = lax.map(spectral_block, (mix_b, dlong_b, taps_b, skip_b))
    longmix = longmix.reshape(D, LENGTH)
    dmix_input = dmix_input.reshape(D, LENGTH)
    filter_grad = filter_grad.reshape(N_TP, GROUPS // N_TP, LENGTH)
    gated_out = (short_out[0].astype(jnp.float32) * longmix.astype(jnp.float32)).astype(jnp.bfloat16)
    block_out = jnp.dot(weight_vals.T, gated_out.astype(jnp.float32), precision=precise).astype(jnp.bfloat16)
    dmix_vals = dmix_input.astype(jnp.float32)
    dshort = jnp.stack([dgated.astype(jnp.float32) * longmix.astype(jnp.float32), dmix_vals * short_out[2].astype(jnp.float32), dmix_vals * short_out[1].astype(jnp.float32)]).astype(jnp.bfloat16)
    proj_grad = jnp.stack([short_stream_grad(dshort[stream_no], conv_weight[:, stream_no]) for stream_no in range(3)])
    return (block_out, proj_grad, filter_grad)
```

```python
import functools
import math

import jax
import jax.numpy as jnp
from jax import lax
from jax.experimental import pallas as pl
from jax.experimental.pallas import tpu as pltpu
from jax.sharding import PartitionSpec as P


def from_behind(block, axis, distance):
    devices = range(lax.axis_size(axis))
    route = [(i - distance, i) for i in devices if i - distance in devices]
    return lax.ppermute(block, axis, route)


def rims(edge_rows, step_by):
    return from_behind(edge_rows, "ctx", step_by)


def short_forward(projected, prev_rim, conv_weight):
    kernel = conv_weight.shape[0]
    tokens = projected.shape[2]
    extended = jnp.concatenate([prev_rim, projected], axis=2)
    summed = jnp.zeros(projected.shape, jnp.float32)
    for offset in range(kernel):
        begin_at = kernel - 1 - offset
        summed = summed + conv_weight[offset][:, :, None] * extended[
            :, :, begin_at : begin_at + tokens
        ].astype(jnp.float32)
    return summed.astype(jnp.bfloat16)


def short_backward(dshort, next_rim, conv_weight):
    kernel = conv_weight.shape[0]
    tokens = dshort.shape[2]
    extended = jnp.concatenate([dshort, next_rim], axis=2)
    summed = jnp.zeros(dshort.shape, jnp.float32)
    for offset in range(kernel):
        summed = summed + conv_weight[offset][:, :, None] * extended[
            :, :, offset : offset + tokens
        ].astype(jnp.float32)
    return summed.astype(jnp.bfloat16)


def to_owners(values_in, ctx_size):
    channels, tokens = values_in.shape
    return lax.all_to_all(
        values_in.reshape(ctx_size, channels // ctx_size, tokens), "ctx", split_axis=0, concat_axis=0, tiled=True
    )


def to_tokens(values_in):
    ctx_size, own_width, tokens = values_in.shape
    arrived = lax.all_to_all(values_in, "ctx", split_axis=0, concat_axis=0, tiled=True)
    return arrived.reshape(ctx_size * own_width, tokens)


BF, F32 = jnp.bfloat16, jnp.float32
NB = 32
OWN = 32
G = 2
T = 128

def dot(a, b, ca, cb):
    return lax.dot_general(a, b, (((ca,), (cb,)), ((), ())), preferred_element_type=F32)

def build_toeplitz(h_ref, hpad, M):
    for g in range(G):
        hpad[g:g + 1, 0:128] = jnp.zeros((1, 128), F32)
        hpad[g:g + 1, 128:] = h_ref[g:g + 1, :]
        M[g, 128:256, 0:128] = jnp.zeros((128, 128), BF)
    def step(e, c):
        for g in range(G):
            seg = hpad[g:g + 1, pl.ds(pl.multiple_of(e * 128, 128), 256)]
            tile = pltpu.roll(jnp.broadcast_to(seg, (128, 256)), 0, 1, stride=1, stride_axis=0)[:, 128:].astype(BF)
            M[g, 0:128, pl.ds(pl.multiple_of(e * 128, 128), 128)] = tile
            M[g, 128:256, pl.ds(pl.multiple_of(e * 128 + 128, 128), 128)] = tile
        return c
    lax.fori_loop(0, NB, step, 0)

def load_pairs(own, X, row0):
    for g in range(G):
        for h in range(2):
            v = own[...].reshape(NB // 2, 2, OWN, T)[:, h, 16 * g:16 * g + 16, :]
            X[g, row0:row0 + 256, T * h:T * h + T] = v.reshape(256, T)

def store_pairs(y, out, g):
    for j in range(NB // 2):
        for h in range(2):
            out[2 * j + h, 16 * g:16 * g + 16, :] = y[16 * j:16 * j + 16, T * h:T * h + T].astype(out.dtype)

def conv_forward(X, M, skip_rows, out):
    for g in range(G):
        acc = jnp.zeros((256, 256), F32)
        for d in range(16):
            acc = acc + dot(X[g, 256 - 16 * d:512 - 16 * d, :], M[g, :, 256 * d:256 * d + 256], 1, 0)
        y = acc + skip_rows(g) * X[g, 256:512, :].astype(F32)
        store_pairs(y, out, g)

def conv_backward(D, M, skip_rows, out):
    for g in range(G):
        acc = jnp.zeros((256, 256), F32)
        for d in range(16):
            acc = acc + dot(D[g, 16 * d:16 * d + 256, :], M[g, :, 256 * d:256 * d + 256], 1, 1)
        y = acc + skip_rows(g) * D[g, 0:256, :].astype(F32)
        store_pairs(y, out, g)

def filter_gradient(X, D, XR, carry, gacc, out, scaling):
    rows = lax.broadcasted_iota(jnp.int32, (256, 256), 0)
    cols = lax.broadcasted_iota(jnp.int32, (256, 256), 1)
    flip = jnp.where(rows + cols == 255, 1.0, 0.0).astype(BF)
    for g in range(G):
        XR[g] = dot(flip, X[g, 256:512, :], 1, 1).astype(BF)
    gacc[...] = jnp.zeros(gacc.shape, F32)
    carry[...] = jnp.zeros(carry.shape, F32)
    def shear(tile):
        wide = jnp.concatenate([tile, jnp.zeros((128, 128), F32)], axis=1)
        return jnp.sum(pltpu.roll(wide, 1, 1, stride=1, stride_axis=0), axis=0, keepdims=True)
    def step(d, c):
        for g in range(G):
            p = dot(XR[g], D[g, pl.ds(pl.multiple_of(16 * d, 16), 256), :], 1, 0)
            at = pl.multiple_of(256 * d, 128)
            gacc[g:g + 1, pl.ds(at, 256)] += shear(p[0:128, 0:128] + carry[g])
            at = pl.multiple_of(256 * d + 128, 128)
            gacc[g:g + 1, pl.ds(at, 256)] += shear(p[0:128, 128:] + p[128:, 0:128])
            carry[g] = p[128:, 128:]
        return c
    lax.fori_loop(0, 16, step, 0)
    for g in range(G):
        last = shear(carry[g])
        gacc[g:g + 1, 4096:4352] += last
        out[g:g + 1, :] = gacc[g:g + 1, 256:4352] * scaling

def skip_of(skip_ref):
    def rows(g):
        s = skip_ref[16 * g:16 * g + 16, :]
        return jnp.broadcast_to(s[None], (16, 16, 256)).reshape(256, 256)
    return rows

SCALE = 1.0 / math.sqrt(16 * 4096)

def kf(own, h, skip, out, hpad, M, X):
    build_toeplitz(h, hpad, M)
    X[:, 0:256, :] = jnp.zeros((G, 256, 256), BF)
    load_pairs(own, X, 256)
    conv_forward(X, M, skip_of(skip), out)

def kb(own, down, h, skip, out, fg, hpad, M, X, D, XR, carry, gacc):
    build_toeplitz(h, hpad, M)
    load_pairs(own, X, 256)
    D[:, 256:512, :] = jnp.zeros((G, 256, 256), BF)
    load_pairs(down, D, 0)
    conv_backward(D, M, skip_of(skip), out)
    filter_gradient(X, D, XR, carry, gacc, fg, SCALE)

HP = pltpu.VMEM((G, 4096 + 128), F32)
MS = pltpu.VMEM((G, 256, 4096 + 128), BF)
XS = pltpu.VMEM((G, 512, 256), BF)

def long_forward(own, h, skip):
    return pl.pallas_call(kf, out_shape=jax.ShapeDtypeStruct((NB, OWN, T), BF),
        scratch_shapes=[HP, MS, XS], compiler_params=pltpu.CompilerParams(vmem_limit_bytes=40 << 20), name="long_forward")(own, h, skip)

def long_backward(own, down, h, skip):
    return pl.pallas_call(kb, out_shape=(jax.ShapeDtypeStruct((NB, OWN, T), BF), jax.ShapeDtypeStruct((G, 4096), F32)),
        scratch_shapes=[HP, MS, XS, XS, pltpu.VMEM((G, 256, 256), BF), pltpu.VMEM((G, 128, 128), F32), pltpu.VMEM((G, 4352), F32)],
        compiler_params=pltpu.CompilerParams(vmem_limit_bytes=40 << 20), name="long_backward")(own, down, h, skip)


def local(projected, conv_weight, filters, skip_gain, out_weight, cotangent):
    kernel = conv_weight.shape[0]
    channels = projected.shape[1]
    tokens = projected.shape[2]
    ctx_size = lax.axis_size("ctx")
    own_width = channels // ctx_size
    weight_full = lax.all_gather(out_weight, "ctx", axis=1, tiled=True)
    prev_rim = rims(projected[:, :, tokens - (kernel - 1) :], 1)
    short_out = short_forward(projected, prev_rim, conv_weight)
    mix_input = (short_out[1].astype(jnp.float32) * short_out[2].astype(jnp.float32)).astype(
        jnp.bfloat16
    )
    weight_cols = weight_full
    dgated = jnp.dot(
        weight_cols,
        lax.all_gather(cotangent, "tp", axis=0, tiled=True),
        preferred_element_type=jnp.float32,
    ).astype(jnp.bfloat16)
    dlongmix = (dgated.astype(jnp.float32) * short_out[0].astype(jnp.float32)).astype(jnp.bfloat16)
    skip_own = lax.dynamic_slice_in_dim(skip_gain, lax.axis_index("ctx") * own_width, own_width)
    own_taps = filters[0]
    mix_own = to_owners(mix_input, ctx_size)
    skip_own = skip_own[:, None]
    long_own = long_forward(mix_own, own_taps, skip_own)
    longmix = to_tokens(long_own)
    dlong_own = to_owners(dlongmix, ctx_size)
    dmix_own, filter_grad = long_backward(mix_own, dlong_own, own_taps, skip_own)
    filter_grad = filter_grad[None]
    dmix_input = to_tokens(dmix_own)
    gated_out = (short_out[0].astype(jnp.float32) * longmix.astype(jnp.float32)).astype(
        jnp.bfloat16
    )
    weight_cols = weight_full
    block_out = lax.psum_scatter(
        lax.dot_general(
            weight_cols, gated_out, (((0,), (0,)), ((), ())), preferred_element_type=jnp.float32
        ).astype(jnp.bfloat16),
        "tp",
        scatter_dimension=0,
        tiled=True,
    )
    dmix_vals = dmix_input.astype(jnp.float32)
    dshort = jnp.stack(
        [
            dgated.astype(jnp.float32) * longmix.astype(jnp.float32),
            dmix_vals * short_out[2].astype(jnp.float32),
            dmix_vals * short_out[1].astype(jnp.float32),
        ]
    ).astype(jnp.bfloat16)
    next_rim = rims(dshort[:, :, : kernel - 1], -1)
    proj_grad = short_backward(dshort, next_rim, conv_weight)
    return (block_out, proj_grad, filter_grad)


def solution(mesh):
    return jax.shard_map(
        local,
        mesh=mesh,
        in_specs=(
            P(None, "tp", "ctx"),
            P(None, None, "tp"),
            P("tp", "ctx", None),
            P("tp"),
            P("tp", "ctx"),
            P("tp", "ctx"),
        ),
        out_specs=(P("tp", "ctx"), P(None, "tp", "ctx"), P("tp", "ctx", None)),
        check_vma=False,
    )
```

```python
import functools
import math

import jax
import jax.numpy as jnp
from jax import lax
from jax.experimental import pallas as pl
from jax.experimental.pallas import tpu as pltpu
from jax.sharding import PartitionSpec as P


def from_behind(block, axis, distance):
    devices = range(lax.axis_size(axis))
    route = [(i - distance, i) for i in devices if i - distance in devices]
    return lax.ppermute(block, axis, route)


def rims(edge_rows, step_by):
    return from_behind(edge_rows, "ctx", step_by)


def short_forward(projected, prev_rim, conv_weight):
    kernel = conv_weight.shape[0]
    tokens = projected.shape[2]
    extended = jnp.concatenate([prev_rim, projected], axis=2)
    summed = jnp.zeros(projected.shape, jnp.float32)
    for offset in range(kernel):
        begin_at = kernel - 1 - offset
        summed = summed + conv_weight[offset][:, :, None] * extended[
            :, :, begin_at : begin_at + tokens
        ].astype(jnp.float32)
    return summed.astype(jnp.bfloat16)


def short_backward(dshort, next_rim, conv_weight):
    kernel = conv_weight.shape[0]
    tokens = dshort.shape[2]
    extended = jnp.concatenate([dshort, next_rim], axis=2)
    summed = jnp.zeros(dshort.shape, jnp.float32)
    for offset in range(kernel):
        summed = summed + conv_weight[offset][:, :, None] * extended[
            :, :, offset : offset + tokens
        ].astype(jnp.float32)
    return summed.astype(jnp.bfloat16)


BF, F32 = jnp.bfloat16, jnp.float32
NB = 32
OWN = 32
G = 2
T = 128

def dot(a, b, ca, cb):
    return lax.dot_general(a, b, (((ca,), (cb,)), ((), ())), preferred_element_type=F32)

def build_toeplitz(h_ref, hpad, M):
    for g in range(G):
        hpad[g:g + 1, 0:128] = jnp.zeros((1, 128), F32)
        hpad[g:g + 1, 128:] = h_ref[g:g + 1, :]
        M[g, 128:256, 0:128] = jnp.zeros((128, 128), BF)
    def step(e, c):
        for g in range(G):
            seg = hpad[g:g + 1, pl.ds(pl.multiple_of(e * 128, 128), 256)]
            tile = pltpu.roll(jnp.broadcast_to(seg, (128, 256)), 0, 1, stride=1, stride_axis=0)[:, 128:].astype(BF)
            M[g, 0:128, pl.ds(pl.multiple_of(e * 128, 128), 128)] = tile
            M[g, 128:256, pl.ds(pl.multiple_of(e * 128 + 128, 128), 128)] = tile
        return c
    lax.fori_loop(0, NB, step, 0)

def load_pairs(own, X, row0):
    for g in range(G):
        for h in range(2):
            v = own[...].reshape(NB // 2, 2, OWN, T)[:, h, 16 * g:16 * g + 16, :]
            X[g, row0:row0 + 256, T * h:T * h + T] = v.reshape(256, T)

def store_pairs(y, out, g):
    for j in range(NB // 2):
        for h in range(2):
            out[2 * j + h, 16 * g:16 * g + 16, :] = y[16 * j:16 * j + 16, T * h:T * h + T].astype(out.dtype)

def conv_forward(X, M, skip_rows, out):
    for g in range(G):
        acc = jnp.zeros((256, 256), F32)
        for d in range(16):
            acc = acc + dot(X[g, 256 - 16 * d:512 - 16 * d, :], M[g, :, 256 * d:256 * d + 256], 1, 0)
        y = acc + skip_rows(g) * X[g, 256:512, :].astype(F32)
        store_pairs(y, out, g)

def conv_backward(D, M, skip_rows, out):
    for g in range(G):
        acc = jnp.zeros((256, 256), F32)
        for d in range(16):
            acc = acc + dot(D[g, 16 * d:16 * d + 256, :], M[g, :, 256 * d:256 * d + 256], 1, 1)
        y = acc + skip_rows(g) * D[g, 0:256, :].astype(F32)
        store_pairs(y, out, g)

def filter_gradient(X, D, XR, carry, gacc, out, scaling):
    rows = lax.broadcasted_iota(jnp.int32, (256, 256), 0)
    cols = lax.broadcasted_iota(jnp.int32, (256, 256), 1)
    flip = jnp.where(rows + cols == 255, 1.0, 0.0).astype(BF)
    for g in range(G):
        XR[g] = dot(flip, X[g, 256:512, :], 1, 1).astype(BF)
    gacc[...] = jnp.zeros(gacc.shape, F32)
    carry[...] = jnp.zeros(carry.shape, F32)
    def shear(tile):
        wide = jnp.concatenate([tile, jnp.zeros((128, 128), F32)], axis=1)
        return jnp.sum(pltpu.roll(wide, 1, 1, stride=1, stride_axis=0), axis=0, keepdims=True)
    def step(d, c):
        for g in range(G):
            p = dot(XR[g], D[g, pl.ds(pl.multiple_of(16 * d, 16), 256), :], 1, 0)
            at = pl.multiple_of(256 * d, 128)
            gacc[g:g + 1, pl.ds(at, 256)] += shear(p[0:128, 0:128] + carry[g])
            at = pl.multiple_of(256 * d + 128, 128)
            gacc[g:g + 1, pl.ds(at, 256)] += shear(p[0:128, 128:] + p[128:, 0:128])
            carry[g] = p[128:, 128:]
        return c
    lax.fori_loop(0, 16, step, 0)
    for g in range(G):
        last = shear(carry[g])
        gacc[g:g + 1, 4096:4352] += last
        out[g:g + 1, :] = gacc[g:g + 1, 256:4352] * scaling

def skip_of(skip_ref):
    def rows(g):
        s = skip_ref[16 * g:16 * g + 16, :]
        return jnp.broadcast_to(s[None], (16, 16, 256)).reshape(256, 256)
    return rows

SCALE = 1.0 / math.sqrt(16 * 4096)

def kf(own, h, skip, out, hpad, M, X):
    build_toeplitz(h, hpad, M)
    X[:, 0:256, :] = jnp.zeros((G, 256, 256), BF)
    load_pairs(own, X, 256)
    conv_forward(X, M, skip_of(skip), out)

def kb(own, down, h, skip, out, fg, hpad, M, X, D, XR, carry, gacc):
    build_toeplitz(h, hpad, M)
    load_pairs(own, X, 256)
    D[:, 256:512, :] = jnp.zeros((G, 256, 256), BF)
    load_pairs(down, D, 0)
    conv_backward(D, M, skip_of(skip), out)
    filter_gradient(X, D, XR, carry, gacc, fg, SCALE)

HP = pltpu.VMEM((G, 4096 + 128), F32)
MS = pltpu.VMEM((G, 256, 4096 + 128), BF)
XS = pltpu.VMEM((G, 512, 256), BF)

def long_forward(own, h, skip):
    return pl.pallas_call(kf, out_shape=jax.ShapeDtypeStruct((NB, OWN, T), BF),
        scratch_shapes=[HP, MS, XS], compiler_params=pltpu.CompilerParams(vmem_limit_bytes=40 << 20), name="long_forward")(own, h, skip)

def long_backward(own, down, h, skip):
    return pl.pallas_call(kb, out_shape=(jax.ShapeDtypeStruct((NB, OWN, T), BF), jax.ShapeDtypeStruct((G, 4096), F32)),
        scratch_shapes=[HP, MS, XS, XS, pltpu.VMEM((G, 256, 256), BF), pltpu.VMEM((G, 128, 128), F32), pltpu.VMEM((G, 4352), F32)],
        compiler_params=pltpu.CompilerParams(vmem_limit_bytes=40 << 20), name="long_backward")(own, down, h, skip)


MESH = pl.DeviceIdType.MESH

def ring_barrier(me):
    sem = pltpu.get_barrier_semaphore()

    def one(k, c):
        pl.semaphore_signal(sem, inc=1, device_id=((me.ctx + k) % 32, me.tp), device_id_type=MESH)
        return c

    lax.fori_loop(1, 32, one, 0)
    pl.semaphore_wait(sem, 31)


def group_barrier(me):
    sem = pltpu.get_barrier_semaphore()
    for same in (1, 0):
        for k in range(same, 4):
            dev = (me.ctx if same else me.partner, (me.tp + k) % 4)
            pl.semaphore_signal(sem, inc=1, device_id=dev, device_id_type=MESH)
    pl.semaphore_wait(sem, 7)


def plane_barrier(me):
    sem = pltpu.get_barrier_semaphore()
    for dx, dz in ((1, 0), (3, 0), (0, 1), (0, 3)):
        dev = (me.at((me.x + dx) % 4, (me.z + dz) % 4), me.tp)
        pl.semaphore_signal(sem, inc=1, device_id=dev, device_id_type=MESH)
    pl.semaphore_wait(sem, 4)


class Place:
    def __init__(self):
        self.ctx = lax.axis_index("ctx"); self.tp = lax.axis_index("tp")
        self.x = self.ctx // 8; self.lo = (self.ctx // 4) % 2; self.z = self.ctx % 4
        self.partner = self.ctx + 4 - 8 * self.lo
    def at(self, x, z):
        return x * 8 + self.lo * 4 + z

def relay(me, w_ref, wg, ssem, rsem):
    x, z = me.x, me.z
    k = [0]
    sends = []
    def send(src, dst, dev):
        c = pltpu.make_async_remote_copy(src_ref=src, dst_ref=dst, send_sem=ssem.at[k[0]], recv_sem=rsem.at[k[0]],
                                         device_id=(dev, me.tp), device_id_type=MESH)
        c.start(); k[0] += 1
        sends.append(c)
        return c
    def geometry(h):
        if h == 0:
            slot = lambda f, s: ((x + s) % 4) * 4 + (z + f) % 4
            dev = lambda f, s: me.at((x + s) % 4, (z + f) % 4)
        else:
            slot = lambda f, s: ((x + f) % 4) * 4 + (z + s) % 4
            dev = lambda f, s: me.at((x + f) % 4, (z + s) % 4)
        return slot, dev, 512 * h
    halves = [geometry(0), geometry(1)]
    def part(ref, slot, r0, n):
        return ref.at[slot, pl.ds(r0, n), :]
    first, second = [None, None], [{}, {}]
    for h in (0, 1):
        slot, dev, r = halves[h]
        src = w_ref.at[pl.ds(r, 512), :]
        first[h] = [send(src, part(wg, slot(0, 0), r, 512), dev(1, 0)), send(src, part(wg, slot(0, 0), r, 512), dev(-1, 0))]
    for h in (0, 1):
        slot, dev, r = halves[h]
        src = w_ref.at[pl.ds(r, 512), :]
        second[h][0] = [send(src, part(wg, slot(0, 0), r, 512), dev(0, 1)), send(src, part(wg, slot(0, 0), r, 512), dev(0, -1))]
    fwd = [[None, None], [None, None]]
    for i, f in ((0, -1), (1, 1)):
        for h in (0, 1):
            slot, dev, r = halves[h]
            first[h][i].wait_recv()
            b = slot(f, 0)
            rr = r + 256 * i
            fwd[h][i] = send(part(wg, b, rr, 256), part(wg, b, rr, 256), dev(-f, 0))
            second[h][f] = [send(part(wg, b, r, 512), part(wg, b, r, 512), dev(0, 1)), send(part(wg, b, r, 512), part(wg, b, r, 512), dev(0, -1))]
    last = []
    def forward2(h, f):
        slot, dev, r = halves[h]
        for i, s in ((0, -1), (1, 1)):
            second[h][f][i].wait_recv()
            b = slot(f, s)
            rr = r + 256 * i
            last.append(send(part(wg, b, rr, 256), part(wg, b, rr, 256), dev(0, -s)))
    for h in (0, 1):
        forward2(h, 0)
    for h in (0, 1):
        slot, dev, r = halves[h]
        for i in (0, 1):
            fwd[h][i].wait_recv()
        b = slot(2, 0)
        second[h][2] = [send(part(wg, b, r, 512), part(wg, b, r, 512), dev(0, 1)), send(part(wg, b, r, 512), part(wg, b, r, 512), dev(0, -1))]
    for f in (-1, 1, 2):
        for h in (0, 1):
            forward2(h, f)
    for c in last:
        c.wait_recv()
    return sends

N_RELAY = 40

def relay_kernel(w_ref, out, ssem, rsem, lsem):
    me = Place()
    own = pltpu.make_async_copy(w_ref, out.at[me.x * 4 + me.z], lsem)
    own.start()
    plane_barrier(me)
    sends = relay(me, w_ref, out, ssem, rsem)
    for c in sends: c.wait_send()
    own.wait()

def a2a_kernel(v_ref, out, ssem, rsem, lsem):
    me = Place()
    own = pltpu.make_async_copy(v_ref.at[me.ctx], out.at[me.ctx], lsem)
    own.start()
    ring_barrier(me)
    def mk(k):
        to = (me.ctx + k) % 32
        return pltpu.make_async_remote_copy(src_ref=v_ref.at[to], dst_ref=out.at[me.ctx], send_sem=ssem.at[k], recv_sem=rsem.at[k],
            device_id=(to, me.tp), device_id_type=MESH)
    def go(k, c): mk(k).start(); return c
    def wt(k, c): mk(k).wait(); return c
    lax.fori_loop(1, 32, go, 0)
    lax.fori_loop(1, 32, wt, 0)
    own.wait()

def ygroup_kernel(v_ref, out, ssem, rsem, lsem):
    me = Place()
    own = pltpu.make_async_copy(v_ref.at[pl.ds(512 * me.lo, 512), :], out.at[me.lo, pl.ds(512 * me.tp, 512), :], lsem)
    own.start()
    group_barrier(me)
    cs = []
    n = 0
    for same in (1, 0):
        for k in range(4):
            if same and k == 0: continue
            lo2 = me.lo if same else 1 - me.lo
            ctx2 = me.ctx if same else me.partner
            c = pltpu.make_async_remote_copy(src_ref=v_ref.at[pl.ds(512 * lo2, 512), :], dst_ref=out.at[me.lo, pl.ds(512 * me.tp, 512), :],
              send_sem=ssem.at[n], recv_sem=rsem.at[n], device_id=(ctx2, (me.tp + k) % 4), device_id_type=MESH)
            c.start(); cs.append(c); n += 1
    for c in cs: c.wait()
    own.wait()


def spread_kernel(v_ref, out, ssem, rsem, lsem):
    me = Place()
    own = pltpu.make_async_copy(v_ref.at[me.lo, me.tp], out.at[me.lo, me.tp], lsem)
    own.start()
    group_barrier(me)
    cs = []
    for same in (1, 0):
        for k in range(same, 4):
            lo2 = me.lo if same else 1 - me.lo
            tp2 = (me.tp + k) % 4
            c = pltpu.make_async_remote_copy(
                src_ref=v_ref.at[lo2, tp2], dst_ref=out.at[me.lo, me.tp], send_sem=ssem.at[len(cs)],
                recv_sem=rsem.at[len(cs)], device_id=(me.ctx if same else me.partner, tp2), device_id_type=MESH)
            c.start()
            cs.append(c)
    for c in cs:
        c.wait()
    own.wait()


def call(kern, out, cid, sems, arg):
    return pl.pallas_call(
        kern, out_shape=jax.ShapeDtypeStruct(out, BF), in_specs=[pl.BlockSpec(memory_space=pltpu.VMEM)],
        out_specs=pl.BlockSpec(memory_space=pltpu.VMEM), name=kern.__name__,
        scratch_shapes=[pltpu.SemaphoreType.DMA((sems,)), pltpu.SemaphoreType.DMA((sems,)), pltpu.SemaphoreType.DMA],
        compiler_params=pltpu.CompilerParams(collective_id=cid, has_side_effects=True, vmem_limit_bytes=32 << 20),
    )(arg)


def to_owners(values_in):
    return call(a2a_kernel, (32, 32, 128), 3, 32, values_in.reshape(32, 32, 128))


def to_tokens(values_in):
    return call(a2a_kernel, (32, 32, 128), 3, 32, values_in).reshape(1024, 128)


def swap(values_in):
    return lax.ppermute(values_in, "ctx", [(i, i ^ 4) for i in range(32)])


def local(projected, conv_weight, filters, skip_gain, out_weight, cotangent):
    kernel = conv_weight.shape[0]
    channels = projected.shape[1]
    tokens = projected.shape[2]
    own_width = OWN
    ctx = lax.axis_index("ctx")
    lo = (ctx // 4) % 2
    weights = call(relay_kernel, (16, 1024, 128), 1, N_RELAY, out_weight)
    cot = call(ygroup_kernel, (2, 2048, 128), 2, 8, cotangent)
    prev_rim = rims(projected[:, :, tokens - (kernel - 1) :], 1)
    short_out = short_forward(projected, prev_rim, conv_weight)
    mix_input = (short_out[1].astype(jnp.float32) * short_out[2].astype(jnp.float32)).astype(
        jnp.bfloat16
    )
    part = jnp.einsum("sco,bsot->bct", weights, cot.reshape(2, 16, 128, 128), preferred_element_type=F32)
    mine = lax.dynamic_index_in_dim(part, lo, 0, False)
    theirs = lax.dynamic_index_in_dim(part, 1 - lo, 0, False).astype(BF)
    dgated = (mine + swap(theirs).astype(F32)).astype(BF)
    dlongmix = (dgated.astype(jnp.float32) * short_out[0].astype(jnp.float32)).astype(jnp.bfloat16)
    skip_own = lax.dynamic_slice_in_dim(skip_gain, ctx * own_width, own_width)[:, None]
    own_taps = filters[0]
    mix_own = to_owners(mix_input)
    longmix = to_tokens(long_forward(mix_own, own_taps, skip_own))
    dlong_own = to_owners(dlongmix)
    dmix_own, filter_grad = long_backward(mix_own, dlong_own, own_taps, skip_own)
    dmix_input = to_tokens(dmix_own)
    gated = (short_out[0].astype(jnp.float32) * longmix.astype(jnp.float32)).astype(jnp.bfloat16)
    other = swap(gated)
    both = jnp.stack([jnp.where(lo == 0, gated, other), jnp.where(lo == 0, other, gated)])
    share = jnp.einsum("bct,pzco->bptzo", both, weights.reshape(4, 4, 1024, 128), preferred_element_type=F32)
    shares = call(spread_kernel, (2, 4, 128, 512), 4, 8, share.astype(BF).reshape(2, 4, 128, 512))
    block_out = jnp.sum(shares.astype(F32), axis=1).transpose(0, 2, 1).reshape(1024, 128).astype(BF)
    dmix_vals = dmix_input.astype(jnp.float32)
    dshort = jnp.stack(
        [
            dgated.astype(jnp.float32) * longmix.astype(jnp.float32),
            dmix_vals * short_out[2].astype(jnp.float32),
            dmix_vals * short_out[1].astype(jnp.float32),
        ]
    ).astype(jnp.bfloat16)
    next_rim = rims(dshort[:, :, : kernel - 1], -1)
    proj_grad = short_backward(dshort, next_rim, conv_weight)
    return (block_out, proj_grad, filter_grad[None])


def solution(mesh):
    return jax.shard_map(
        local,
        mesh=mesh,
        in_specs=(
            P(None, "tp", "ctx"),
            P(None, None, "tp"),
            P("tp", "ctx", None),
            P("tp"),
            P("tp", "ctx"),
            P("tp", "ctx"),
        ),
        out_specs=(P("tp", "ctx"), P(None, "tp", "ctx"), P("tp", "ctx", None)),
        check_vma=False,
    )
```

```python
import math

import jax
import jax.numpy as jnp
from jax import lax
from jax.experimental import pallas as pl
from jax.experimental.pallas import tpu as pltpu
from jax.sharding import PartitionSpec as P

BF, F32 = jnp.bfloat16, jnp.float32
MESH = pl.DeviceIdType.MESH
NB = 32
OWN = 32
G = 2
T = 128
C = 1024
TAPS = 7
SCALE = 1.0 / math.sqrt(16 * 4096)


def dot(a, b, ca, cb):
    return lax.dot_general(a, b, (((ca,), (cb,)), ((), ())), preferred_element_type=F32)


def at(value, multiple):
    return pl.multiple_of(value, multiple)


def build_toeplitz(h_ref, hpad, M):
    for g in range(G):
        hpad[g:g + 1, 0:128] = jnp.zeros((1, 128), F32)
        hpad[g:g + 1, 128:] = h_ref[g:g + 1, :]
        M[g, 128:256, 0:128] = jnp.zeros((128, 128), BF)
    def step(e, c):
        for g in range(G):
            seg = hpad[g:g + 1, pl.ds(pl.multiple_of(e * 128, 128), 256)]
            tile = pltpu.roll(jnp.broadcast_to(seg, (128, 256)), 0, 1, stride=1, stride_axis=0)[:, 128:].astype(BF)
            M[g, 0:128, pl.ds(pl.multiple_of(e * 128, 128), 128)] = tile
            M[g, 128:256, pl.ds(pl.multiple_of(e * 128 + 128, 128), 128)] = tile
        return c
    lax.fori_loop(0, NB, step, 0)


def load_pairs(own, X, row0):
    for g in range(G):
        for h in range(2):
            v = own[...].reshape(NB // 2, 2, OWN, T)[:, h, 16 * g:16 * g + 16, :]
            X[g, row0:row0 + 256, T * h:T * h + T] = v.reshape(256, T)


def store_pairs(y, out, g):
    for j in range(NB // 2):
        for h in range(2):
            out[2 * j + h, 16 * g:16 * g + 16, :] = y[16 * j:16 * j + 16, T * h:T * h + T].astype(out.dtype)


def conv_forward(X, M, skip_rows, out):
    for g in range(G):
        acc = jnp.zeros((256, 256), F32)
        for d in range(16):
            acc = acc + dot(X[g, 256 - 16 * d:512 - 16 * d, :], M[g, :, 256 * d:256 * d + 256], 1, 0)
        y = acc + skip_rows(g) * X[g, 256:512, :].astype(F32)
        store_pairs(y, out, g)


def conv_backward(D, M, skip_rows, out):
    for g in range(G):
        acc = jnp.zeros((256, 256), F32)
        for d in range(16):
            acc = acc + dot(D[g, 16 * d:16 * d + 256, :], M[g, :, 256 * d:256 * d + 256], 1, 1)
        y = acc + skip_rows(g) * D[g, 0:256, :].astype(F32)
        store_pairs(y, out, g)


def filter_gradient(X, D, XR, carry, gacc, out, scaling):
    rows = lax.broadcasted_iota(jnp.int32, (256, 256), 0)
    cols = lax.broadcasted_iota(jnp.int32, (256, 256), 1)
    flip = jnp.where(rows + cols == 255, 1.0, 0.0).astype(BF)
    for g in range(G):
        XR[g] = dot(flip, X[g, 256:512, :], 1, 1).astype(BF)
    gacc[...] = jnp.zeros(gacc.shape, F32)
    carry[...] = jnp.zeros(carry.shape, F32)
    def shear(tile):
        wide = jnp.concatenate([tile, jnp.zeros((128, 128), F32)], axis=1)
        return jnp.sum(pltpu.roll(wide, 1, 1, stride=1, stride_axis=0), axis=0, keepdims=True)
    def step(d, c):
        for g in range(G):
            p = dot(XR[g], D[g, pl.ds(pl.multiple_of(16 * d, 16), 256), :], 1, 0)
            at = pl.multiple_of(256 * d, 128)
            gacc[g:g + 1, pl.ds(at, 256)] += shear(p[0:128, 0:128] + carry[g])
            at = pl.multiple_of(256 * d + 128, 128)
            gacc[g:g + 1, pl.ds(at, 256)] += shear(p[0:128, 128:] + p[128:, 0:128])
            carry[g] = p[128:, 128:]
        return c
    lax.fori_loop(0, 16, step, 0)
    for g in range(G):
        last = shear(carry[g])
        gacc[g:g + 1, 4096:4352] += last
        out[g:g + 1, :] = gacc[g:g + 1, 256:4352] * scaling

class Place:
    def __init__(self):
        self.ctx = lax.axis_index("ctx")
        self.tp = lax.axis_index("tp")
        self.x = self.ctx // 8
        self.lo = (self.ctx // 4) % 2
        self.z = self.ctx % 4
        self.partner = self.ctx + 4 - 8 * self.lo

    def plane(self, x, z):
        return x * 8 + self.lo * 4 + z


def barrier_signals(me):
    sem = pltpu.get_barrier_semaphore()

    def one(k, c):
        pl.semaphore_signal(sem, inc=1, device_id=((me.ctx + k) % NB, me.tp), device_id_type=MESH)
        return c

    lax.fori_loop(1, NB, one, 0)
    for k in (1, 2, 3):
        for ctx in (me.ctx, me.partner):
            pl.semaphore_signal(sem, inc=1, device_id=(ctx, (me.tp + k) % 4), device_id_type=MESH)
    return sem


class Relay:
    def __init__(self, me, w, wg, ssem, rsem):
        self.me, self.w, self.wg, self.ssem, self.rsem = me, w, wg, ssem, rsem
        self.sends = []
        self.first = [None, None]
        self.fwd = [[None, None], [None, None]]
        self.second = [{}, {}]
        self.last = [{}, {}]

    def slot(self, h, f, s):
        me = self.me
        if h == 0:
            return ((me.x + s) % 4) * 4 + (me.z + f) % 4
        return ((me.x + f) % 4) * 4 + (me.z + s) % 4

    def dev(self, h, f, s):
        me = self.me
        if h == 0:
            return me.plane((me.x + s) % 4, (me.z + f) % 4)
        return me.plane((me.x + f) % 4, (me.z + s) % 4)

    def send(self, src, dst, dev):
        n = len(self.sends)
        c = pltpu.make_async_remote_copy(
            src_ref=src, dst_ref=dst, send_sem=self.ssem.at[n], recv_sem=self.rsem.at[n],
            device_id=(dev, self.me.tp), device_id_type=MESH)
        c.start()
        self.sends.append(c)
        return c

    def part(self, b, r, n):
        return self.wg.at[b, pl.ds(r, n), :]

    def own(self, h):
        return self.w.at[pl.ds(512 * h, 512), :]

    def pair(self, h, f):
        b = self.slot(h, f, 0)
        dst = self.part(b, 512 * h, 512)
        src = self.own(h) if f == 0 else dst
        self.second[h][f] = [self.send(src, dst, self.dev(h, 0, 1)), self.send(src, dst, self.dev(h, 0, -1))]

    def begin(self):
        for h in (0, 1):
            dst = self.part(self.slot(h, 0, 0), 512 * h, 512)
            self.first[h] = [self.send(self.own(h), dst, self.dev(h, 1, 0)), self.send(self.own(h), dst, self.dev(h, -1, 0))]
        for h in (0, 1):
            self.pair(h, 0)

    def neighbours(self):
        for i, f in ((0, -1), (1, 1)):
            for h in (0, 1):
                self.first[h][i].wait_recv()
                part = self.part(self.slot(h, f, 0), 512 * h + 256 * i, 256)
                self.fwd[h][i] = self.send(part, part, self.dev(h, -f, 0))
                self.pair(h, f)

    def opposite(self):
        for h in (0, 1):
            for i in (0, 1):
                self.fwd[h][i].wait_recv()
            self.pair(h, 2)

    def forward(self, h, f):
        cs = []
        for i, s in ((0, -1), (1, 1)):
            self.second[h][f][i].wait_recv()
            part = self.part(self.slot(h, f, s), 512 * h + 256 * i, 256)
            cs.append(self.send(part, part, self.dev(h, 0, -s)))
        self.last[h][f] = cs

    def finish(self, h, f):
        for c in self.last[h][f]:
            c.wait_recv()


class Exchange:
    def __init__(self, me, src, dst, ssem, rsem):
        self.me, self.src, self.dst, self.ssem, self.rsem = me, src, dst, ssem, rsem

    def send(self, to):
        pltpu.make_async_remote_copy(
            src_ref=self.src.at[to], dst_ref=self.dst.at[self.me.ctx], send_sem=self.ssem, recv_sem=self.rsem,
            device_id=(to, self.me.tp), device_id_type=MESH).start()

    def start(self):
        def go(k, c):
            self.send((self.me.ctx + k) % NB)
            return c

        lax.fori_loop(1, NB, go, 0)
        self.dst[self.me.ctx] = self.src[self.me.ctx]

    def all(self):
        return pltpu.make_async_remote_copy(
            src_ref=self.src.at[pl.ds(0, NB - 1)], dst_ref=self.dst.at[pl.ds(0, NB - 1)], send_sem=self.ssem,
            recv_sem=self.rsem, device_id=(self.me.partner, self.me.tp), device_id_type=MESH)


def group_copies(me, pick, dst, ssem, rsem):
    cs = []
    for same in (1, 0):
        for k in range(same, 4):
            lo = me.lo if same else 1 - me.lo
            tp = (me.tp + k) % 4
            cs.append(pltpu.make_async_remote_copy(
                src_ref=pick(lo, tp), dst_ref=dst, send_sem=ssem.at[len(cs)], recv_sem=rsem.at[len(cs)],
                device_id=(me.ctx if same else me.partner, tp), device_id_type=MESH))
    return cs


def lanes(shape):
    return lax.broadcasted_iota(jnp.int32, shape, len(shape) - 1)


def picker(first):
    rows = lax.broadcasted_iota(jnp.int32, (16, T), 0)
    return jnp.where(lanes((16, T)) == rows + first, 1.0, 0.0).astype(BF)


def taps_to_rows(cw, cwt):
    for b in range(C // T):
        rows = [cw[j, s:s + 1, T * b:T * b + T] for j in range(TAPS) for s in range(3)]
        block = jnp.concatenate(rows + [jnp.zeros((T - len(rows), T), F32)], axis=0)
        cwt[T * b:T * b + T, :] = block.T


def short_rows(s, rows, x, rim, cwt, backward):
    lane = lanes((T, T))
    total = cwt[rows, s:s + 1] * x
    for j in range(1, TAPS):
        if backward:
            shifted = pltpu.roll(jnp.where(lane < j, rim, x), T - j, 1)
        else:
            shifted = pltpu.roll(jnp.where(lane >= T - j, rim, x), j, 1)
        total = total + cwt[rows, 3 * j + s:3 * j + s + 1] * shifted
    return total


def kernel(proj, cw, filt, skip, w, cot, block_out, proj_grad, filter_grad,
           wg, cotg, rim_s, rim_r, short, mix_s, mix_r, long_s, long_r, gated, acc, part_s, part_r, dgated,
           dlong_s, dlong_r, dmix_s, dmix_r, dshort, share_s, share_r, cwt, hpad, M, X, D, XR, carry, gacc,
           relay_ss, relay_rs, x_ss, x_rs, cot_ss, cot_rs, share_ss, share_rs, rim_ss, rim_rs, part_ss, part_rs,
           gated_ss, gated_rs):
    me = Place()
    sem = barrier_signals(me)
    ahead, behind = (me.ctx + 1) % NB, (me.ctx + NB - 1) % NB

    def rim_copy(n, streams, to):
        return pltpu.make_async_remote_copy(
            src_ref=rim_s.at[streams], dst_ref=rim_r.at[streams], send_sem=rim_ss.at[n], recv_sem=rim_rs.at[n],
            device_id=(to, me.tp), device_id_type=MESH)

    last16, first16 = picker(T - 16), picker(0)
    for s in range(3):
        rim_s[s] = dot(last16, proj[s], 1, 1).astype(BF)
    pl.semaphore_wait(sem, NB - 1 + 6)

    relay = Relay(me, w, wg, relay_ss, relay_rs)
    rim0 = rim_copy(0, pl.ds(0, 3), ahead)
    rim0.start()
    relay.begin()
    cots = group_copies(me, lambda lo, tp: cot.at[pl.ds(at(512 * lo, 512), 512), :],
                        cotg.at[me.lo, pl.ds(at(512 * me.tp, 512), 512), :], cot_ss, cot_rs)
    for c in cots:
        c.start()

    wg[me.x * 4 + me.z] = w[...]
    cotg[me.lo, pl.ds(at(512 * me.tp, 512), 512), :] = cot[pl.ds(at(512 * me.lo, 512), 512), :]
    taps_to_rows(cw, cwt)
    build_toeplitz(filt, hpad, M)
    X[:, 0:256, :] = jnp.zeros((G, 256, 256), BF)
    D[:, 256:512, :] = jnp.zeros((G, 256, 256), BF)
    own_rows = lax.broadcasted_iota(jnp.int32, (OWN, C), 0) + me.ctx * OWN
    skip_own = jnp.sum(jnp.where(lanes((OWN, C)) == own_rows, skip[...], 0.0), axis=1, keepdims=True)

    def skip_rows(g):
        return jnp.broadcast_to(skip_own[None, 16 * g:16 * g + 16, :], (16, 16, 256)).reshape(256, 256)

    rim0.wait_recv()

    def short_step(r, c):
        rows = pl.ds(at(T * r, T), T)
        outs = []
        for s in range(3):
            rim = dot(rim_r[s, :, rows], last16, 0, 0)
            rim = jnp.where(me.ctx == 0, 0.0, rim)
            out = short_rows(s, rows, proj[s, rows, :].astype(F32), rim, cwt, False).astype(BF)
            short[s, rows, :] = out
            outs.append(out)
        mix = (outs[1].astype(F32) * outs[2].astype(F32)).astype(BF)
        mix_s[pl.ds(4 * r, 4)] = mix.reshape(4, OWN, T)
        return c

    lax.fori_loop(0, C // T, short_step, 0)
    relay.neighbours()
    mix_x = Exchange(me, mix_s, mix_r, x_ss.at[0], x_rs.at[0])
    mix_x.start()
    for h in (0, 1):
        relay.forward(h, 0)
    relay.opposite()

    mix_x.all().wait_recv()
    load_pairs(mix_r, X, 256)
    conv_forward(X, M, skip_rows, long_s)
    long_x = Exchange(me, long_s, long_r, x_ss.at[1], x_rs.at[1])
    long_x.start()
    for h in (0, 1):
        relay.forward(h, -1)
    for h in (0, 1):
        relay.forward(h, 1)
    for c in cots:
        c.wait_recv()

    def slots(h, f):
        me_f = (me.z + f) % 4 if h == 0 else (me.x + f) % 4
        return [(k * 4 + me_f) if h == 0 else (me_f * 4 + k) for k in range(4)]

    def columns(h, f):
        found = slots(h, f)
        return jnp.concatenate([
            jnp.concatenate([cotg[b, pl.ds(at(s * T, T), T), :] for s in found], axis=0) for b in (0, 1)], axis=1)

    def partial(h, f, r):
        left = jnp.concatenate([wg[s, r:r + 256, :] for s in slots(h, f)], axis=1)
        return left

    def contract(h, f, first):
        right = columns(h, f)
        for r in (512 * h, 512 * h + 256):
            value = dot(partial(h, f, r), right, 1, 0)
            if first:
                acc[r:r + 256, :] = value
            else:
                acc[r:r + 256, :] += value

    long_x.all().wait_recv()

    def gated_step(r, c):
        rows = pl.ds(at(T * r, T), T)
        value = short[0, rows, :].astype(F32) * long_r[pl.ds(4 * r, 4)].reshape(T, T).astype(F32)
        gated[me.lo, :, rows] = value.T.astype(BF)
        return c

    lax.fori_loop(0, C // T, gated_step, 0)
    gated_c = pltpu.make_async_remote_copy(
        src_ref=gated.at[me.lo], dst_ref=gated.at[me.lo], send_sem=gated_ss, recv_sem=gated_rs,
        device_id=(me.partner, me.tp), device_id_type=MESH)
    gated_c.start()
    for h in (0, 1):
        relay.forward(h, 2)
    for n, f in enumerate((0, -1, 1)):
        for h in (0, 1):
            relay.finish(h, f)
            contract(h, f, n == 0)

    parts = []
    for h in (0, 1):
        relay.finish(h, 2)
        right = columns(h, 2)
        for r in (512 * h, 512 * h + 256):
            value = acc[r:r + 256, :] + dot(partial(h, 2, r), right, 1, 0)
            theirs = jnp.where(me.lo == 0, value[:, T:], value[:, :T])
            part_s[r:r + 256, :] = theirs.astype(BF)
            n = len(parts)
            c = pltpu.make_async_remote_copy(
                src_ref=part_s.at[pl.ds(r, 256), :], dst_ref=part_r.at[pl.ds(r, 256), :], send_sem=part_ss.at[n],
                recv_sem=part_rs.at[n], device_id=(me.partner, me.tp), device_id_type=MESH)
            c.start()
            parts.append(c)
            acc[r:r + 256, 0:T] = jnp.where(me.lo == 0, value[:, :T], value[:, T:])

    dlong_x = Exchange(me, dlong_s, dlong_r, x_ss.at[2], x_rs.at[2])
    for n in range(4):
        parts[n].wait_recv()
        r = 256 * n
        value = (acc[r:r + 256, 0:T] + part_r[r:r + 256, :].astype(F32)).astype(BF)
        dgated[r:r + 256, :] = value
        value = (value.astype(F32) * short[0, r:r + 256, :].astype(F32)).astype(BF)
        dlong_s[8 * n:8 * n + 8] = value.reshape(8, OWN, T)
    dlong_x.start()

    def dq_step(r, c):
        rows = pl.ds(at(T * r, T), T)
        value = dgated[rows, :].astype(F32) * long_r[pl.ds(4 * r, 4)].reshape(T, T).astype(F32)
        dshort[0, rows, :] = value.astype(BF)
        return c

    lax.fori_loop(0, C // T, dq_step, 0)
    rim_s[3] = dot(first16, dshort[0], 1, 1).astype(BF)
    rim1 = rim_copy(1, pl.ds(3, 1), behind)
    rim1.start()

    gated_c.wait_recv()
    left = gated[...].reshape(2 * T, C)
    for x in range(4):
        for p in (0, 1):
            right = jnp.concatenate([wg[4 * x + 2 * p], wg[4 * x + 2 * p + 1]], axis=1)
            value = dot(left, right, 1, 0).astype(BF)
            for b in (0, 1):
                share_s[b, x, :, 256 * p:256 * p + 256] = value[T * b:T * b + T, :]
    share_r[me.lo, me.tp] = share_s[me.lo, me.tp]

    def grad_step(s):
        def step(r, c):
            rows = pl.ds(at(T * r, T), T)
            rim = dot(rim_r[3 + s, :, rows], first16, 0, 0)
            rim = jnp.where(me.ctx == NB - 1, 0.0, rim)
            out = short_rows(s, rows, dshort[s, rows, :].astype(F32), rim, cwt, True)
            proj_grad[s, rows, :] = out.astype(BF)
            return c
        return step

    dlong_x.all().wait_recv()
    shares = group_copies(me, lambda lo, tp: share_s.at[lo, tp], share_r.at[me.lo, me.tp], share_ss, share_rs)
    for c in shares:
        c.start()
    load_pairs(dlong_r, D, 0)
    conv_backward(D, M, skip_rows, dmix_s)
    dmix_x = Exchange(me, dmix_s, dmix_r, x_ss.at[3], x_rs.at[3])
    dmix_x.start()
    filter_gradient(X, D, XR, carry, gacc, filter_grad, SCALE)
    rim1.wait_recv()
    lax.fori_loop(0, C // T, grad_step(0), 0)

    dmix_x.all().wait_recv()

    def dkv_step(r, c):
        rows = pl.ds(at(T * r, T), T)
        value = dmix_r[pl.ds(4 * r, 4)].reshape(T, T).astype(F32)
        for s in (1, 2):
            dshort[s, rows, :] = (value * short[3 - s, rows, :].astype(F32)).astype(BF)
        return c

    lax.fori_loop(0, C // T, dkv_step, 0)
    for s in (1, 2):
        rim_s[3 + s] = dot(first16, dshort[s], 1, 1).astype(BF)
    rim2 = rim_copy(2, pl.ds(4, 2), behind)
    rim2.start()
    for c in shares:
        c.wait_recv()
    for b in (0, 1):
        for k in range(4):
            cols = slice(T * k, T * k + T)
            value = share_r[b, 0, :, cols].astype(F32)
            for tp in (1, 2, 3):
                value = value + share_r[b, tp, :, cols].astype(F32)
            block_out[512 * b + T * k:512 * b + T * k + T, :] = value.T.astype(BF)
    rim2.wait_recv()
    for s in (1, 2):
        lax.fori_loop(0, C // T, grad_step(s), 0)
    for c in [rim0, rim1, rim2, gated_c] + relay.sends + cots + parts + shares:
        c.wait_send()
    for x in (mix_x, long_x, dlong_x, dmix_x):
        x.all().wait_send()


def local(projected, conv_weight, filters, skip_gain, out_weight, cotangent):
    dma = pltpu.SemaphoreType.DMA
    vmem = pltpu.VMEM
    blocks = vmem((NB, OWN, T), BF)
    rows = vmem((C, T), BF)
    scratch = dict(
        wg=vmem((16, C, T), BF), cotg=vmem((2, 2048, T), BF), rim_s=vmem((6, 16, C), BF), rim_r=vmem((6, 16, C), BF),
        short=vmem((3, C, T), BF), mix_s=blocks, mix_r=blocks, long_s=blocks, long_r=blocks, gated=vmem((2, T, C), BF),
        acc=vmem((C, 2 * T), F32), part_s=rows, part_r=rows, dgated=rows, dlong_s=blocks, dlong_r=blocks, dmix_s=blocks,
        dmix_r=blocks, dshort=vmem((3, C, T), BF), share_s=vmem((2, 4, T, 512), BF), share_r=vmem((2, 4, T, 512), BF),
        cwt=vmem((C, T), F32), hpad=vmem((G, 4096 + T), F32), M=vmem((G, 256, 4096 + T), BF), X=vmem((G, 512, 256), BF),
        D=vmem((G, 512, 256), BF), XR=vmem((G, 256, 256), BF), carry=vmem((G, T, T), F32), gacc=vmem((G, 4352), F32),
        relay_ss=dma((40,)), relay_rs=dma((40,)), x_ss=dma((4,)), x_rs=dma((4,)), cot_ss=dma((7,)), cot_rs=dma((7,)),
        share_ss=dma((7,)), share_rs=dma((7,)), rim_ss=dma((3,)), rim_rs=dma((3,)), part_ss=dma((4,)), part_rs=dma((4,)),
        gated_ss=dma, gated_rs=dma)
    whole = pl.BlockSpec(memory_space=pltpu.VMEM)
    block_out, proj_grad, filter_grad = pl.pallas_call(
        kernel,
        out_shape=(
            jax.ShapeDtypeStruct((C, T), BF),
            jax.ShapeDtypeStruct((3, C, T), BF),
            jax.ShapeDtypeStruct((G, 4096), F32),
        ),
        in_specs=[whole] * 6,
        out_specs=(whole,) * 3,
        scratch_shapes=list(scratch.values()),
        compiler_params=pltpu.CompilerParams(collective_id=1, has_side_effects=True, vmem_limit_bytes=48 << 20),
        name="hyena_block",
    )(projected, conv_weight, filters[0], skip_gain[None], out_weight, cotangent)
    return block_out, proj_grad, filter_grad[None]


def solution(mesh):
    return jax.shard_map(
        local,
        mesh=mesh,
        in_specs=(
            P(None, "tp", "ctx"),
            P(None, None, "tp"),
            P("tp", "ctx", None),
            P("tp"),
            P("tp", "ctx"),
            P("tp", "ctx"),
        ),
        out_specs=(P("tp", "ctx"), P(None, "tp", "ctx"), P("tp", "ctx", None)),
        check_vma=False,
    )
```

```python
import math

import jax
import jax.numpy as jnp
from jax import lax
from jax.experimental import pallas as pl
from jax.experimental.pallas import tpu as pltpu
from jax.sharding import PartitionSpec as P

BF, F32 = jnp.bfloat16, jnp.float32
MESH = pl.DeviceIdType.MESH
NB = 32
OWN = 32
G = 2
T = 128
C = 1024
TAPS = 7
SCALE = 1.0 / math.sqrt(16 * 4096)


def dot(a, b, ca, cb):
    return lax.dot_general(a, b, (((ca,), (cb,)), ((), ())), preferred_element_type=F32)


def at(value, multiple):
    return pl.multiple_of(value, multiple)


def build_toeplitz(h_ref, hpad, M):
    for g in range(G):
        hpad[g:g + 1, 0:128] = jnp.zeros((1, 128), F32)
        hpad[g:g + 1, 128:] = h_ref[g:g + 1, :]
        M[g, 128:256, 0:128] = jnp.zeros((128, 128), BF)
    def step(e, c):
        for g in range(G):
            seg = hpad[g:g + 1, pl.ds(pl.multiple_of(e * 128, 128), 256)]
            tile = pltpu.roll(jnp.broadcast_to(seg, (128, 256)), 0, 1, stride=1, stride_axis=0)[:, 128:].astype(BF)
            M[g, 0:128, pl.ds(pl.multiple_of(e * 128, 128), 128)] = tile
            M[g, 128:256, pl.ds(pl.multiple_of(e * 128 + 128, 128), 128)] = tile
        return c
    lax.fori_loop(0, NB, step, 0)


def load_pairs(own, X, row0):
    for g in range(G):
        for h in range(2):
            v = own[...].reshape(NB // 2, 2, OWN, T)[:, h, 16 * g:16 * g + 16, :]
            X[g, row0:row0 + 256, T * h:T * h + T] = v.reshape(256, T)


def store_pairs(y, out, g):
    for j in range(NB // 2):
        for h in range(2):
            out[2 * j + h, 16 * g:16 * g + 16, :] = y[16 * j:16 * j + 16, T * h:T * h + T].astype(out.dtype)


def conv_forward(X, M, skip_rows, out):
    for g in range(G):
        acc = jnp.zeros((256, 256), F32)
        for d in range(16):
            acc = acc + dot(X[g, 256 - 16 * d:512 - 16 * d, :], M[g, :, 256 * d:256 * d + 256], 1, 0)
        y = acc + skip_rows(g) * X[g, 256:512, :].astype(F32)
        store_pairs(y, out, g)


def conv_backward(D, M, skip_rows, out):
    for g in range(G):
        acc = jnp.zeros((256, 256), F32)
        for d in range(16):
            acc = acc + dot(D[g, 16 * d:16 * d + 256, :], M[g, :, 256 * d:256 * d + 256], 1, 1)
        y = acc + skip_rows(g) * D[g, 0:256, :].astype(F32)
        store_pairs(y, out, g)


def filter_gradient(X, D, XR, carry, gacc, out, scaling):
    rows = lax.broadcasted_iota(jnp.int32, (256, 256), 0)
    cols = lax.broadcasted_iota(jnp.int32, (256, 256), 1)
    flip = jnp.where(rows + cols == 255, 1.0, 0.0).astype(BF)
    for g in range(G):
        XR[g] = dot(flip, X[g, 256:512, :], 1, 1).astype(BF)
    gacc[...] = jnp.zeros(gacc.shape, F32)
    carry[...] = jnp.zeros(carry.shape, F32)
    def shear(tile):
        wide = jnp.concatenate([tile, jnp.zeros((128, 128), F32)], axis=1)
        return jnp.sum(pltpu.roll(wide, 1, 1, stride=1, stride_axis=0), axis=0, keepdims=True)
    def step(d, c):
        for g in range(G):
            p = dot(XR[g], D[g, pl.ds(pl.multiple_of(16 * d, 16), 256), :], 1, 0)
            at = pl.multiple_of(256 * d, 128)
            gacc[g:g + 1, pl.ds(at, 256)] += shear(p[0:128, 0:128] + carry[g])
            at = pl.multiple_of(256 * d + 128, 128)
            gacc[g:g + 1, pl.ds(at, 256)] += shear(p[0:128, 128:] + p[128:, 0:128])
            carry[g] = p[128:, 128:]
        return c
    lax.fori_loop(0, 16, step, 0)
    for g in range(G):
        last = shear(carry[g])
        gacc[g:g + 1, 4096:4352] += last
        out[g:g + 1, :] = gacc[g:g + 1, 256:4352] * scaling


class Place:
    def __init__(self):
        self.ctx = lax.axis_index("ctx")
        self.tp = lax.axis_index("tp")
        self.x = self.ctx // 8
        self.lo = (self.ctx // 4) % 2
        self.z = self.ctx % 4
        self.hi = self.tp // 2
        self.core = self.tp % 2
        self.partner = self.ctx + 4 - 8 * self.lo
        self.sibling = self.tp + 1 - 2 * self.core
        self.across = (self.tp + 2) % 4

    def plane(self, x, z):
        return x * 8 + self.lo * 4 + z

    def group(self):
        return [(self.ctx, self.across), (self.partner, self.tp), (self.partner, self.across)]


def barrier_signals(me):
    sem = pltpu.get_barrier_semaphore()

    def one(k, c):
        pl.semaphore_signal(sem, inc=1, device_id=((me.ctx + k) % NB, me.tp), device_id_type=MESH)
        return c

    lax.fori_loop(1, NB, one, 0)
    for dev in ((me.ctx, me.sibling), (me.ctx, me.across), (me.partner, me.across)):
        pl.semaphore_signal(sem, inc=1, device_id=dev, device_id_type=MESH)
    return sem


def remote(src, dst, ssem, rsem, dev):
    return pltpu.make_async_remote_copy(
        src_ref=src, dst_ref=dst, send_sem=ssem, recv_sem=rsem, device_id=dev, device_id_type=MESH)


class Relay:
    def __init__(self, me, w, wg, ssem, rsem):
        self.me, self.w, self.wg, self.ssem, self.rsem = me, w, wg, ssem, rsem
        self.sends = []
        self.first = [None, None]
        self.fwd = [[None, None], [None, None]]
        self.second = [{}, {}]
        self.last = [{}, {}]

    def slot(self, h, f, s):
        me = self.me
        if h == 0:
            return ((me.x + s) % 4) * 4 + (me.z + f) % 4
        return ((me.x + f) % 4) * 4 + (me.z + s) % 4

    def dev(self, h, f, s):
        me = self.me
        if h == 0:
            return me.plane((me.x + s) % 4, (me.z + f) % 4)
        return me.plane((me.x + f) % 4, (me.z + s) % 4)

    def send(self, src, dst, dev):
        n = len(self.sends)
        c = remote(src, dst, self.ssem.at[n], self.rsem.at[n], (dev, self.me.tp))
        c.start()
        self.sends.append(c)
        return c

    def part(self, b, r, n):
        return self.wg.at[b, pl.ds(r, n), :]

    def own(self, h):
        return self.w.at[pl.ds(512 * h, 512), :]

    def pair(self, h, f):
        b = self.slot(h, f, 0)
        dst = self.part(b, 512 * h, 512)
        src = self.own(h) if f == 0 else dst
        self.second[h][f] = [self.send(src, dst, self.dev(h, 0, 1)), self.send(src, dst, self.dev(h, 0, -1))]

    def begin(self):
        for h in (0, 1):
            dst = self.part(self.slot(h, 0, 0), 512 * h, 512)
            self.first[h] = [self.send(self.own(h), dst, self.dev(h, 1, 0)), self.send(self.own(h), dst, self.dev(h, -1, 0))]

    def neighbours(self):
        for i, f in ((0, -1), (1, 1)):
            for h in (0, 1):
                self.first[h][i].wait_recv()
                part = self.part(self.slot(h, f, 0), 512 * h + 256 * i, 256)
                self.fwd[h][i] = self.send(part, part, self.dev(h, -f, 0))
                self.pair(h, f)

    def opposite(self):
        for h in (0, 1):
            for i in (0, 1):
                self.fwd[h][i].wait_recv()
            self.pair(h, 2)

    def forward(self, h, f):
        cs = []
        for i, s in ((0, -1), (1, 1)):
            self.second[h][f][i].wait_recv()
            part = self.part(self.slot(h, f, s), 512 * h + 256 * i, 256)
            cs.append(self.send(part, part, self.dev(h, 0, -s)))
        self.last[h][f] = cs

    def finish(self, h, f):
        for c in self.last[h][f]:
            c.wait_recv()


class Exchange:
    def __init__(self, me, src, dst, whole, sems):
        self.me, self.src, self.dst, self.whole, self.sems = me, src, dst, whole, sems

    def start(self):
        def go(k, c):
            to = (self.me.ctx + k) % NB
            remote(self.src(to), self.dst, self.sems[0], self.sems[1], (to, self.me.tp)).start()
            return c

        lax.fori_loop(1, NB, go, 0)

    def all(self):
        return remote(self.whole, self.whole, self.sems[0], self.sems[1], (self.me.partner, self.me.tp))


def lanes(shape):
    return lax.broadcasted_iota(jnp.int32, shape, len(shape) - 1)


def shift_matrix(SH, backward):
    for j in range(1, TAPS):
        rows = lax.broadcasted_iota(jnp.int32, (2 * T, T), 0)
        col = lanes((2 * T, T))
        source = col + j if backward else (col + (2 * T - j)) % (2 * T)
        SH[:, T * (j - 1):T * j] = jnp.where(rows == source, 1.0, 0.0).astype(BF)


def own_taps(me, cw, skip, taps, spread):
    at_block = pl.ds(at((me.ctx // 4) * T, T), T)
    rows = [cw[j, s:s + 1, at_block] for j in range(TAPS) for s in range(3)] + [skip[:, at_block]]
    rows = jnp.concatenate(rows + [jnp.zeros((T - len(rows), T), F32)], axis=0)
    taps[...] = rows.T
    own = taps[pl.ds(at((me.ctx % 4) * OWN, OWN), OWN), :]
    for n in range(3 * TAPS + 1):
        spread[n] = jnp.broadcast_to(own[:, n:n + 1], (OWN, T))


def short_conv(s, x, beside, SH, spread, blocks):
    both = jnp.concatenate([x, beside], axis=1)
    total = x.reshape(blocks, OWN, T).astype(F32) * spread[s][None]
    for p in range(3):
        moved = dot(both, SH[:, 2 * T * p:2 * T * p + 2 * T], 1, 0)
        for i in (0, 1):
            j = 2 * p + i + 1
            total = total + moved[:, T * i:T * i + T].reshape(blocks, OWN, T) * spread[3 * j + s][None]
    return total


def kernel(proj, cw_in, filt_in, skip_in, w, cot, block_out, proj_grad, filter_grad,
           cw, filt, skip, taps, spread, SF, SB, pr, wg, cotg, short, mix, longm, gated_s, gated_r, gated_t, acc,
           dgated_s, dgated_r, dmix, dshort, grad, share_s, sib_r, pre_s, share_r, hpad, M, X, D, XR, carry, gacc,
           local_s, relay_ss, relay_rs, x_ss, x_rs, cot_ss, cot_rs, pass_ss, pass_rs, sib_ss, sib_rs, share_ss, share_rs):
    me = Place()
    sem = barrier_signals(me)
    BLK = 8
    mine = pl.ds(at(OWN * me.ctx, OWN), OWN)
    half = pl.ds(at(512 * me.tp, 512), 512)

    def class_rows(lo):
        return cot.at[pl.ds(at(512 * lo, 512), 512), :]

    loads = [(cw_in, cw), (filt_in, filt), (skip_in, skip), (w, wg.at[me.x * 4 + me.z]),
             (class_rows(me.lo), cotg.at[me.lo, half, :]), (proj.at[:, mine, :], pr.at[me.ctx + 1])]
    loads = [pltpu.make_async_copy(a, b, local_s.at[n]) for n, (a, b) in enumerate(loads)]
    for c in loads:
        c.start()
    shift_matrix(SF, False)
    shift_matrix(SB, True)
    pr[0] = jnp.zeros((3, OWN, T), BF)
    for s in range(3):
        dshort[s, NB] = jnp.zeros((OWN, T), BF)
    X[:, 0:256, :] = jnp.zeros((G, 256, 256), BF)
    D[:, 256:512, :] = jnp.zeros((G, 256, 256), BF)
    pl.semaphore_wait(sem, NB - 1 + 3)

    relay = Relay(me, w, wg, relay_ss, relay_rs)
    relay.begin()
    cots = []
    for n, (ctx, tp) in enumerate(me.group()):
        lo = me.lo if n == 0 else 1 - me.lo
        cots.append(remote(class_rows(lo), cotg.at[me.lo, half, :], cot_ss.at[n], cot_rs.at[n], (ctx, tp)))
        cots[n].start()
    passes = [remote(class_rows(me.lo), cotg.at[me.lo, half, :], pass_ss.at[3], pass_rs.at[3], (me.ctx, me.sibling))]
    passes[0].start()
    for h in (0, 1):
        relay.pair(h, 0)
    proj_x = Exchange(me, lambda to: proj.at[:, pl.ds(at(OWN * to, OWN), OWN), :], pr.at[me.ctx + 1],
                      pr.at[pl.ds(1, NB - 1)], (x_ss.at[0], x_rs.at[0]))
    proj_x.start()

    for c in loads[:3]:
        c.wait()
    own_taps(me, cw, skip, taps, spread)
    build_toeplitz(filt, hpad, M)

    def skip_rows(g):
        s = spread[3 * TAPS][16 * g:16 * g + 16, :]
        s = jnp.concatenate([s, s], axis=1)
        return jnp.broadcast_to(s[None], (16, 16, 256)).reshape(256, 256)

    relay.neighbours()
    across = pl.ds(at(512 * me.across, 512), 512)
    came = [(me.lo, across), (1 - me.lo, half), (1 - me.lo, across)]
    for n, (lo, rows) in enumerate(came):
        cots[n].wait_recv()
        part = cotg.at[lo, rows, :]
        c = remote(part, part, pass_ss.at[n], pass_rs.at[n], (me.ctx, me.sibling))
        c.start()
        passes.append(c)
    for h in (0, 1):
        relay.forward(h, 0)
    relay.opposite()

    for c in loads[3:]:
        c.wait()
    proj_x.all().wait_recv()

    def short_step(r, c):
        outs = []
        for s in range(3):
            x = pr[pl.ds(BLK * r + 1, BLK), s].reshape(BLK * OWN, T)
            before = pr[pl.ds(BLK * r, BLK), s].reshape(BLK * OWN, T)
            out = short_conv(s, x, before, SF, spread, BLK).astype(BF)
            short[s, pl.ds(BLK * r, BLK)] = out
            outs.append(out.astype(F32))
        mix[pl.ds(BLK * r, BLK)] = (outs[1] * outs[2]).astype(BF)
        return c

    lax.fori_loop(0, NB // BLK, short_step, 0)
    for f in (-1, 1):
        for h in (0, 1):
            relay.forward(h, f)

    load_pairs(mix, X, 256)
    conv_forward(X, M, skip_rows, longm)
    for x in range(4):
        for b in (0, 1):
            for z in range(4):
                n = 8 * x + 4 * b + z
                gated_s[4 * x + z, b] = (short[0, n].astype(F32) * longm[n].astype(F32)).astype(BF)
    for h in (0, 1):
        relay.forward(h, 2)
    gated_x = Exchange(me, lambda to: gated_s.at[(to // 8) * 4 + to % 4], gated_r.at[me.ctx],
                       gated_r.at[pl.ds(0, NB - 1)], (x_ss.at[1], x_rs.at[1]))
    gated_x.start()
    gated_r[me.ctx] = gated_s[me.x * 4 + me.z]
    for c in passes:
        c.wait_recv()

    def slots(h, f):
        if h == 0:
            return [k * 4 + (me.z + f) % 4 for k in range(4)]
        return [((me.x + f) % 4) * 4 + k for k in range(4)]

    def product(h, f, r, right):
        left = jnp.concatenate([wg[s, r:r + 256, :] for s in slots(h, f)], axis=1)
        return dot(left, right, 1, 0)

    def columns(h, f):
        return jnp.concatenate([
            jnp.concatenate([cotg[b, pl.ds(at(s * T, T), T), :] for s in slots(h, f)], axis=0) for b in (0, 1)], axis=1)

    for f in (0, -1, 1, 2):
        for h in (0, 1):
            relay.finish(h, f)
            right = columns(h, f)
            for r in (512 * h, 512 * h + 256):
                value = product(h, f, r, right)
                if f != 0:
                    value = value + acc[r:r + 256, :]
                if f != 2:
                    acc[r:r + 256, :] = value
                    continue
                for b in (0, 1):
                    dgated_s[r // OWN:r // OWN + 8, b] = value[:, T * b:T * b + T].astype(BF).reshape(8, OWN, T)
    dgated_x = Exchange(me, lambda to: dgated_s.at[to], dgated_r.at[me.ctx], dgated_r.at[pl.ds(0, NB - 1)],
                        (x_ss.at[2], x_rs.at[2]))
    dgated_x.start()
    dgated_r[me.ctx] = dgated_s[me.ctx]

    gated_x.all().wait_recv()
    for b in (0, 1):
        for k in range(C // T):
            block = gated_r[4 * k:4 * k + 4, b].reshape(T, T).astype(F32)
            gated_t[T * b:T * b + T, T * k:T * k + T] = block.T.astype(BF)
    for x in range(4):
        for p in (0, 1):
            right = jnp.concatenate([wg[4 * x + 2 * p], wg[4 * x + 2 * p + 1]], axis=1)
            value = dot(gated_t[...], right, 1, 0).astype(BF)
            for b in (0, 1):
                share_s[x % 2, b, x // 2, :, 256 * p:256 * p + 256] = value[T * b:T * b + T, :]
    sib = remote(share_s.at[1 - me.core], sib_r, sib_ss, sib_rs, (me.ctx, me.sibling))
    sib.start()
    sib.wait_recv()
    for b in (0, 1):
        for hi in (0, 1):
            value = share_s[me.core, b, hi].astype(F32) + sib_r[b, hi].astype(F32)
            pre_s[b, hi] = value.astype(BF)
    shares = []
    for n, (ctx, tp) in enumerate(me.group()):
        b = me.lo if n == 0 else 1 - me.lo
        hi = me.hi if n == 1 else 1 - me.hi
        shares.append(remote(pre_s.at[b, hi], share_r.at[me.lo, me.hi], share_ss.at[n], share_rs.at[n], (ctx, tp)))
        shares[n].start()
    share_r[me.lo, me.hi] = pre_s[me.lo, me.hi]

    dgated_x.all().wait_recv()
    for n in range(NB):
        b, pair = (n // 4) % 2, n - n % 8 + n % 4
        value = (dgated_r[pair, b].astype(F32) + dgated_r[pair + 4, b].astype(F32)).astype(BF).astype(F32)
        dlong = (value * short[0, n].astype(F32)).astype(BF)
        for g in range(G):
            row = 16 * (n // 2)
            D[g, row:row + 16, T * (n % 2):T * (n % 2) + T] = dlong[16 * g:16 * g + 16, :]
        dshort[0, n] = (value * longm[n].astype(F32)).astype(BF)

    def grad_of(s):
        def step(r, c):
            x = dshort[s, pl.ds(BLK * r, BLK)].reshape(BLK * OWN, T)
            after = dshort[s, pl.ds(BLK * r + 1, BLK)].reshape(BLK * OWN, T)
            grad[s, pl.ds(BLK * r, BLK)] = short_conv(s, x, after, SB, spread, BLK).astype(BF)
            return c

        lax.fori_loop(0, NB // BLK, step, 0)
        moved = Exchange(me, lambda to: grad.at[s, to], proj_grad.at[s, mine, :],
                         proj_grad.at[s, pl.ds(0, C - OWN), :], (x_ss.at[3 + s], x_rs.at[3 + s]))
        moved.start()
        own = pltpu.make_async_copy(grad.at[s, me.ctx], proj_grad.at[s, mine, :], local_s.at[6 + s])
        own.start()
        return moved, own

    grads = [grad_of(0)]
    conv_backward(D, M, skip_rows, dmix)

    def dkv_step(r, c):
        at_r = pl.ds(BLK * r, BLK)
        value = dmix[at_r].astype(F32)
        for s in (1, 2):
            dshort[s, at_r] = (value * short[3 - s, at_r].astype(F32)).astype(BF)
        return c

    lax.fori_loop(0, NB // BLK, dkv_step, 0)
    grads.append(grad_of(1))
    grads.append(grad_of(2))

    filter_gradient(X, D, XR, carry, gacc, filter_grad, SCALE)
    for c in shares:
        c.wait_recv()
    for b in (0, 1):
        for k in range(4):
            cols = slice(T * k, T * k + T)
            value = share_r[b, 0, :, cols].astype(F32) + share_r[b, 1, :, cols].astype(F32)
            block_out[512 * b + T * k:512 * b + T * k + T, :] = value.T.astype(BF)
    for c in relay.sends + cots + passes + [sib] + shares:
        c.wait_send()
    for x in (proj_x, gated_x, dgated_x):
        x.all().wait_send()
    for moved, own in grads:
        own.wait()
        moved.all().wait_send()
        moved.all().wait_recv()


def local(projected, conv_weight, filters, skip_gain, out_weight, cotangent):
    dma = pltpu.SemaphoreType.DMA
    vmem = pltpu.VMEM
    blocks = vmem((NB, OWN, T), BF)
    pairs = vmem((NB, 2, OWN, T), BF)
    shares = vmem((2, 2, T, 512), BF)
    scratch = dict(
        cw=vmem((TAPS, 3, C), F32), filt=vmem((G, 4096), F32), skip=vmem((1, C), F32), taps=vmem((T, T), F32),
        spread=vmem((3 * TAPS + 1, OWN, T), F32), SF=vmem((2 * T, 6 * T), BF), SB=vmem((2 * T, 6 * T), BF),
        pr=vmem((NB + 1, 3, OWN, T), BF), wg=vmem((16, C, T), BF), cotg=vmem((2, 2048, T), BF),
        short=vmem((3, NB, OWN, T), BF), mix=blocks, longm=blocks, gated_s=vmem((16, 2, OWN, T), BF), gated_r=pairs,
        gated_t=vmem((2 * T, C), BF), acc=vmem((C, 2 * T), F32), dgated_s=pairs, dgated_r=pairs, dmix=blocks,
        dshort=vmem((3, NB + 1, OWN, T), BF), grad=vmem((3, NB, OWN, T), BF), share_s=vmem((2, 2, 2, T, 512), BF),
        sib_r=shares, pre_s=shares, share_r=shares, hpad=vmem((G, 4096 + T), F32), M=vmem((G, 256, 4096 + T), BF),
        X=vmem((G, 512, 256), BF), D=vmem((G, 512, 256), BF), XR=vmem((G, 256, 256), BF), carry=vmem((G, T, T), F32),
        gacc=vmem((G, 4352), F32), local_s=dma((9,)),
        relay_ss=dma((40,)), relay_rs=dma((40,)), x_ss=dma((6,)), x_rs=dma((6,)), cot_ss=dma((3,)), cot_rs=dma((3,)),
        pass_ss=dma((4,)), pass_rs=dma((4,)), sib_ss=dma, sib_rs=dma, share_ss=dma((3,)), share_rs=dma((3,)))
    anywhere = pl.BlockSpec(memory_space=pl.ANY)
    whole = pl.BlockSpec(memory_space=pltpu.VMEM)
    block_out, proj_grad, filter_grad = pl.pallas_call(
        kernel,
        out_shape=(
            jax.ShapeDtypeStruct((C, T), BF),
            jax.ShapeDtypeStruct((3, C, T), BF),
            jax.ShapeDtypeStruct((G, 4096), F32),
        ),
        in_specs=[anywhere] * 6,
        out_specs=(whole, anywhere, whole),
        scratch_shapes=list(scratch.values()),
        compiler_params=pltpu.CompilerParams(collective_id=1, has_side_effects=True, vmem_limit_bytes=60 << 20),
        name="hyena_block",
    )(projected, conv_weight, filters[0], skip_gain[None], out_weight, cotangent)
    return block_out, proj_grad, filter_grad[None]


def solution(mesh):
    return jax.shard_map(
        local,
        mesh=mesh,
        in_specs=(
            P(None, "tp", "ctx"),
            P(None, None, "tp"),
            P("tp", "ctx", None),
            P("tp"),
            P("tp", "ctx"),
            P("tp", "ctx"),
        ),
        out_specs=(P("tp", "ctx"), P(None, "tp", "ctx"), P("tp", "ctx", None)),
        check_vma=False,
    )
```

```python
import math

import jax
import jax.numpy as jnp
from jax import lax
from jax.experimental import pallas as pl
from jax.experimental.pallas import tpu as pltpu
from jax.sharding import PartitionSpec as P

BF, F32 = jnp.bfloat16, jnp.float32
MESH = pl.DeviceIdType.MESH
NB = 32
OWN = 32
G = 2
T = 128
C = 1024
TAPS = 7
SCALE = 1.0 / math.sqrt(16 * 4096)


def dot(a, b, ca, cb):
    return lax.dot_general(a, b, (((ca,), (cb,)), ((), ())), preferred_element_type=F32)


def at(value, multiple):
    return pl.multiple_of(value, multiple)


def build_toeplitz(h_ref, hpad, M):
    for g in range(G):
        hpad[g:g + 1, 0:128] = jnp.zeros((1, 128), F32)
        hpad[g:g + 1, 128:] = h_ref[g:g + 1, :]
        M[g, 128:256, 0:128] = jnp.zeros((128, 128), BF)
    def step(e, c):
        for g in range(G):
            seg = hpad[g:g + 1, pl.ds(pl.multiple_of(e * 128, 128), 256)]
            tile = pltpu.roll(jnp.broadcast_to(seg, (128, 256)), 0, 1, stride=1, stride_axis=0)[:, 128:].astype(BF)
            M[g, 0:128, pl.ds(pl.multiple_of(e * 128, 128), 128)] = tile
            M[g, 128:256, pl.ds(pl.multiple_of(e * 128 + 128, 128), 128)] = tile
        return c
    lax.fori_loop(0, NB, step, 0)


def load_pairs(own, X, row0):
    for g in range(G):
        for h in range(2):
            v = own[...].reshape(NB // 2, 2, OWN, T)[:, h, 16 * g:16 * g + 16, :]
            X[g, row0:row0 + 256, T * h:T * h + T] = v.reshape(256, T)


def store_pairs(y, out, g):
    for j in range(NB // 2):
        for h in range(2):
            out[2 * j + h, 16 * g:16 * g + 16, :] = y[16 * j:16 * j + 16, T * h:T * h + T].astype(out.dtype)


def conv_forward(X, M, skip_rows, out):
    for g in range(G):
        acc = jnp.zeros((256, 256), F32)
        for d in range(16):
            acc = acc + dot(X[g, 256 - 16 * d:512 - 16 * d, :], M[g, :, 256 * d:256 * d + 256], 1, 0)
        y = acc + skip_rows(g) * X[g, 256:512, :].astype(F32)
        store_pairs(y, out, g)


def conv_backward(D, M, skip_rows, out):
    for g in range(G):
        acc = jnp.zeros((256, 256), F32)
        for d in range(16):
            acc = acc + dot(D[g, 16 * d:16 * d + 256, :], M[g, :, 256 * d:256 * d + 256], 1, 1)
        y = acc + skip_rows(g) * D[g, 0:256, :].astype(F32)
        store_pairs(y, out, g)


def filter_gradient(X, D, XR, carry, gacc, out, scaling):
    rows = lax.broadcasted_iota(jnp.int32, (256, 256), 0)
    cols = lax.broadcasted_iota(jnp.int32, (256, 256), 1)
    flip = jnp.where(rows + cols == 255, 1.0, 0.0).astype(BF)
    for g in range(G):
        XR[g] = dot(flip, X[g, 256:512, :], 1, 1).astype(BF)
    gacc[...] = jnp.zeros(gacc.shape, F32)
    carry[...] = jnp.zeros(carry.shape, F32)
    def shear(tile):
        wide = jnp.concatenate([tile, jnp.zeros((128, 128), F32)], axis=1)
        return jnp.sum(pltpu.roll(wide, 1, 1, stride=1, stride_axis=0), axis=0, keepdims=True)
    def step(d, c):
        for g in range(G):
            p = dot(XR[g], D[g, pl.ds(pl.multiple_of(16 * d, 16), 256), :], 1, 0)
            at = pl.multiple_of(256 * d, 128)
            gacc[g:g + 1, pl.ds(at, 256)] += shear(p[0:128, 0:128] + carry[g])
            at = pl.multiple_of(256 * d + 128, 128)
            gacc[g:g + 1, pl.ds(at, 256)] += shear(p[0:128, 128:] + p[128:, 0:128])
            carry[g] = p[128:, 128:]
        return c
    lax.fori_loop(0, 16, step, 0)
    for g in range(G):
        last = shear(carry[g])
        gacc[g:g + 1, 4096:4352] += last
        out[g:g + 1, :] = gacc[g:g + 1, 256:4352] * scaling


class Place:
    def __init__(self):
        self.ctx = lax.axis_index("ctx")
        self.tp = lax.axis_index("tp")
        self.x = self.ctx // 8
        self.lo = (self.ctx // 4) % 2
        self.z = self.ctx % 4
        self.hi = self.tp // 2
        self.core = self.tp % 2
        self.partner = self.ctx + 4 - 8 * self.lo
        self.sibling = self.tp + 1 - 2 * self.core
        self.across = (self.tp + 2) % 4

    def plane(self, x, z):
        return x * 8 + self.lo * 4 + z

    def group(self):
        return [(self.ctx, self.across), (self.partner, self.tp), (self.partner, self.across)]


def barrier_signals(me):
    sem = pltpu.get_barrier_semaphore()

    def one(k, c):
        pl.semaphore_signal(sem, inc=1, device_id=((me.ctx + k) % NB, me.tp), device_id_type=MESH)
        return c

    lax.fori_loop(1, NB, one, 0)
    for dev in ((me.ctx, me.sibling), (me.ctx, me.across), (me.partner, me.across)):
        pl.semaphore_signal(sem, inc=1, device_id=dev, device_id_type=MESH)
    return sem


def remote(src, dst, ssem, rsem, dev):
    return pltpu.make_async_remote_copy(
        src_ref=src, dst_ref=dst, send_sem=ssem, recv_sem=rsem, device_id=dev, device_id_type=MESH)


class Relay:
    def __init__(self, me, w, wg, ssem, rsem):
        self.me, self.w, self.wg, self.ssem, self.rsem = me, w, wg, ssem, rsem
        self.sends = []
        self.first = [None, None]
        self.fwd = [[None, None], [None, None]]
        self.second = [{}, {}]
        self.last = [{}, {}]

    def slot(self, h, f, s):
        me = self.me
        if h == 0:
            return ((me.x + s) % 4) * 4 + (me.z + f) % 4
        return ((me.x + f) % 4) * 4 + (me.z + s) % 4

    def dev(self, h, f, s):
        me = self.me
        if h == 0:
            return me.plane((me.x + s) % 4, (me.z + f) % 4)
        return me.plane((me.x + f) % 4, (me.z + s) % 4)

    def send(self, src, dst, dev):
        n = len(self.sends)
        c = remote(src, dst, self.ssem.at[n], self.rsem.at[n], (dev, self.me.tp))
        c.start()
        self.sends.append(c)
        return c

    def part(self, b, r, n):
        return self.wg.at[b, pl.ds(r, n), :]

    def own(self, h):
        return self.w.at[pl.ds(512 * h, 512), :]

    def pair(self, h, f):
        b = self.slot(h, f, 0)
        dst = self.part(b, 512 * h, 512)
        src = self.own(h) if f == 0 else dst
        self.second[h][f] = [self.send(src, dst, self.dev(h, 0, 1)), self.send(src, dst, self.dev(h, 0, -1))]

    def begin(self):
        for h in (0, 1):
            dst = self.part(self.slot(h, 0, 0), 512 * h, 512)
            self.first[h] = [self.send(self.own(h), dst, self.dev(h, 1, 0)), self.send(self.own(h), dst, self.dev(h, -1, 0))]

    def neighbours(self):
        for i, f in ((0, -1), (1, 1)):
            for h in (0, 1):
                self.first[h][i].wait_recv()
                part = self.part(self.slot(h, f, 0), 512 * h + 256 * i, 256)
                self.fwd[h][i] = self.send(part, part, self.dev(h, -f, 0))
                self.pair(h, f)

    def opposite(self):
        for h in (0, 1):
            for i in (0, 1):
                self.fwd[h][i].wait_recv()
            self.pair(h, 2)

    def forward(self, h, f):
        cs = []
        for i, s in ((0, -1), (1, 1)):
            self.second[h][f][i].wait_recv()
            part = self.part(self.slot(h, f, s), 512 * h + 256 * i, 256)
            cs.append(self.send(part, part, self.dev(h, 0, -s)))
        self.last[h][f] = cs

    def finish(self, h, f):
        for c in self.last[h][f]:
            c.wait_recv()


class Exchange:
    def __init__(self, me, src, dst, whole, sems):
        self.me, self.src, self.dst, self.whole, self.sems = me, src, dst, whole, sems

    def start(self):
        def go(k, c):
            to = (self.me.ctx + k) % NB
            remote(self.src(to), self.dst, self.sems[0], self.sems[1], (to, self.me.tp)).start()
            return c

        lax.fori_loop(1, NB, go, 0)

    def all(self):
        return remote(self.whole, self.whole, self.sems[0], self.sems[1], (self.me.partner, self.me.tp))


def lanes(shape):
    return lax.broadcasted_iota(jnp.int32, shape, len(shape) - 1)


def shift_matrix(SH, backward):
    for j in range(1, TAPS):
        rows = lax.broadcasted_iota(jnp.int32, (2 * T, T), 0)
        col = lanes((2 * T, T))
        source = col + j if backward else (col + (2 * T - j)) % (2 * T)
        SH[:, T * (j - 1):T * j] = jnp.where(rows == source, 1.0, 0.0).astype(BF)


def own_taps(me, cw, skip, taps, spread):
    at_block = pl.ds(at((me.ctx // 4) * T, T), T)
    rows = [cw[s, j:j + 1, at_block] for j in range(TAPS) for s in range(3)] + [skip[:, at_block]]
    rows = jnp.concatenate(rows + [jnp.zeros((T - len(rows), T), F32)], axis=0)
    taps[...] = rows.T
    own = taps[pl.ds(at((me.ctx % 4) * OWN, OWN), OWN), :]
    for n in range(3 * TAPS + 1):
        spread[n] = jnp.broadcast_to(own[:, n:n + 1], (OWN, T))


def short_conv(s, x, beside, SH, spread, blocks):
    both = jnp.concatenate([x, beside], axis=1)
    total = x.reshape(blocks, OWN, T).astype(F32) * spread[s][None]
    for p in range(3):
        moved = dot(both, SH[:, 2 * T * p:2 * T * p + 2 * T], 1, 0)
        for i in (0, 1):
            j = 2 * p + i + 1
            total = total + moved[:, T * i:T * i + T].reshape(blocks, OWN, T) * spread[3 * j + s][None]
    return total


def kernel(proj, cw_in, filt_in, skip_in, w, cot, block_out, proj_grad, filter_grad,
           cw, filt, skip, taps, spread, SF, SB, pr, wg, cotg, short, mix, longm, gated_s, gated_r, gated_t, acc,
           dgated_s, dgated_r, dmix, dshort, grad, share_s, sib_r, pre_s, share_r, hpad, M, X, D, XR, carry, gacc,
           local_s, relay_ss, relay_rs, x_ss, x_rs, cot_ss, cot_rs, pass_ss, pass_rs, sib_ss, sib_rs, share_ss, share_rs):
    me = Place()
    sem = barrier_signals(me)
    BLK = 8
    mine = pl.ds(at(OWN * me.ctx, OWN), OWN)
    half = pl.ds(at(512 * me.tp, 512), 512)

    def class_rows(lo):
        return cot.at[pl.ds(at(512 * lo, 512), 512), :]

    loads = [(cw_in, cw), (filt_in, filt), (skip_in, skip), (w, wg.at[me.x * 4 + me.z]),
             (class_rows(me.lo), cotg.at[me.lo, half, :]), (proj.at[:, mine, :], pr.at[me.ctx + 1])]
    loads = [pltpu.make_async_copy(a, b, local_s.at[n]) for n, (a, b) in enumerate(loads)]
    for c in loads:
        c.start()
    shift_matrix(SF, False)
    shift_matrix(SB, True)
    pr[0] = jnp.zeros((3, OWN, T), BF)
    for s in range(3):
        dshort[s, NB] = jnp.zeros((OWN, T), BF)
    X[:, 0:256, :] = jnp.zeros((G, 256, 256), BF)
    D[:, 256:512, :] = jnp.zeros((G, 256, 256), BF)
    pl.semaphore_wait(sem, NB - 1 + 3)

    relay = Relay(me, w, wg, relay_ss, relay_rs)
    relay.begin()
    cots = []
    for n, (ctx, tp) in enumerate(me.group()):
        lo = me.lo if n == 0 else 1 - me.lo
        cots.append(remote(class_rows(lo), cotg.at[me.lo, half, :], cot_ss.at[n], cot_rs.at[n], (ctx, tp)))
        cots[n].start()
    passes = [remote(class_rows(me.lo), cotg.at[me.lo, half, :], pass_ss.at[3], pass_rs.at[3], (me.ctx, me.sibling))]
    passes[0].start()
    for h in (0, 1):
        relay.pair(h, 0)
    def skip_rows(g):
        s = spread[3 * TAPS][16 * g:16 * g + 16, :]
        s = jnp.concatenate([s, s], axis=1)
        return jnp.broadcast_to(s[None], (16, 16, 256)).reshape(256, 256)

    def slots(h, f):
        if h == 0:
            return [k * 4 + (me.z + f) % 4 for k in range(4)]
        return [((me.x + f) % 4) * 4 + k for k in range(4)]

    def product(h, f, r, right):
        left = jnp.concatenate([wg[s, r:r + 256, :] for s in slots(h, f)], axis=1)
        return dot(left, right, 1, 0)

    def columns(h, f):
        return jnp.concatenate([
            jnp.concatenate([cotg[b, pl.ds(at(s * T, T), T), :] for s in slots(h, f)], axis=0) for b in (0, 1)], axis=1)

    def contract(f):
        for h in (0, 1):
            relay.finish(h, f)
            right = columns(h, f)
            for r in (512 * h, 512 * h + 256):
                value = product(h, f, r, right)
                if f != 0:
                    value = value + acc[r:r + 256, :]
                if f != 2:
                    acc[r:r + 256, :] = value
                    continue
                for b in (0, 1):
                    dgated_s[r // OWN:r // OWN + 8, b] = value[:, T * b:T * b + T].astype(BF).reshape(8, OWN, T)

    proj_x = Exchange(me, lambda to: proj.at[:, pl.ds(at(OWN * to, OWN), OWN), :], pr.at[me.ctx + 1],
                      pr.at[pl.ds(1, NB - 1)], (x_ss.at[0], x_rs.at[0]))
    proj_x.start()
    for c in loads[:3]:
        c.wait()
    own_taps(me, cw, skip, taps, spread)
    relay.neighbours()
    build_toeplitz(filt, hpad, M)
    for h in (0, 1):
        relay.forward(h, 0)
    relay.opposite()
    for c in loads[3:]:
        c.wait()
    proj_x.all().wait_recv()

    def short_step(r, c):
        outs = []
        for s in range(3):
            x = pr[pl.ds(BLK * r + 1, BLK), s].reshape(BLK * OWN, T)
            before = pr[pl.ds(BLK * r, BLK), s].reshape(BLK * OWN, T)
            out = short_conv(s, x, before, SF, spread, BLK).astype(BF)
            short[s, pl.ds(BLK * r, BLK)] = out
            outs.append(out.astype(F32))
        mix[pl.ds(BLK * r, BLK)] = (outs[1] * outs[2]).astype(BF)
        return c

    lax.fori_loop(0, NB // BLK, short_step, 0)
    across = pl.ds(at(512 * me.across, 512), 512)
    came = [(me.lo, across), (1 - me.lo, half), (1 - me.lo, across)]
    for n, (lo, rows) in enumerate(came):
        cots[n].wait_recv()
        part = cotg.at[lo, rows, :]
        c = remote(part, part, pass_ss.at[n], pass_rs.at[n], (me.ctx, me.sibling))
        c.start()
        passes.append(c)
    for h in (0, 1):
        relay.forward(h, -1)
    load_pairs(mix, X, 256)
    conv_forward(X, M, skip_rows, longm)
    for x in range(4):
        for b in (0, 1):
            for z in range(4):
                n = 8 * x + 4 * b + z
                gated_s[4 * x + z, b] = (short[0, n].astype(F32) * longm[n].astype(F32)).astype(BF)
    for h in (0, 1):
        relay.forward(h, 1)
    gated_x = Exchange(me, lambda to: gated_s.at[(to // 8) * 4 + to % 4], gated_r.at[me.ctx],
                       gated_r.at[pl.ds(0, NB - 1)], (x_ss.at[1], x_rs.at[1]))
    gated_x.start()
    gated_r[me.ctx] = gated_s[me.x * 4 + me.z]
    for c in passes:
        c.wait_recv()
    contract(0)
    for h in (0, 1):
        relay.forward(h, 2)
    contract(-1)
    contract(1)
    contract(2)
    dgated_x = Exchange(me, lambda to: dgated_s.at[to], dgated_r.at[me.ctx], dgated_r.at[pl.ds(0, NB - 1)],
                        (x_ss.at[2], x_rs.at[2]))
    dgated_x.start()
    dgated_r[me.ctx] = dgated_s[me.ctx]

    gated_x.all().wait_recv()
    for b in (0, 1):
        for k in range(C // T):
            block = gated_r[4 * k:4 * k + 4, b].reshape(T, T).astype(F32)
            gated_t[T * b:T * b + T, T * k:T * k + T] = block.T.astype(BF)
    for x in range(4):
        for p in (0, 1):
            right = jnp.concatenate([wg[4 * x + 2 * p], wg[4 * x + 2 * p + 1]], axis=1)
            value = dot(gated_t[...], right, 1, 0).astype(BF)
            for b in (0, 1):
                share_s[x % 2, b, x // 2, :, 256 * p:256 * p + 256] = value[T * b:T * b + T, :]
    sib = remote(share_s.at[1 - me.core], sib_r, sib_ss, sib_rs, (me.ctx, me.sibling))
    sib.start()
    sib.wait_recv()
    for b in (0, 1):
        for hi in (0, 1):
            value = share_s[me.core, b, hi].astype(F32) + sib_r[b, hi].astype(F32)
            pre_s[b, hi] = value.astype(BF)
    shares = []
    for n, (ctx, tp) in enumerate(me.group()):
        b = me.lo if n == 0 else 1 - me.lo
        hi = me.hi if n == 1 else 1 - me.hi
        shares.append(remote(pre_s.at[b, hi], share_r.at[me.lo, me.hi], share_ss.at[n], share_rs.at[n], (ctx, tp)))
        shares[n].start()
    share_r[me.lo, me.hi] = pre_s[me.lo, me.hi]

    dgated_x.all().wait_recv()
    for n in range(NB):
        b, pair = (n // 4) % 2, n - n % 8 + n % 4
        value = (dgated_r[pair, b].astype(F32) + dgated_r[pair + 4, b].astype(F32)).astype(BF).astype(F32)
        dlong = (value * short[0, n].astype(F32)).astype(BF)
        for g in range(G):
            row = 16 * (n // 2)
            D[g, row:row + 16, T * (n % 2):T * (n % 2) + T] = dlong[16 * g:16 * g + 16, :]
        dshort[0, n] = (value * longm[n].astype(F32)).astype(BF)

    def grad_of(s):
        def step(r, c):
            x = dshort[s, pl.ds(BLK * r, BLK)].reshape(BLK * OWN, T)
            after = dshort[s, pl.ds(BLK * r + 1, BLK)].reshape(BLK * OWN, T)
            grad[s, pl.ds(BLK * r, BLK)] = short_conv(s, x, after, SB, spread, BLK).astype(BF)
            return c

        lax.fori_loop(0, NB // BLK, step, 0)
        moved = Exchange(me, lambda to: grad.at[s, to], proj_grad.at[s, mine, :],
                         proj_grad.at[s, pl.ds(0, C - OWN), :], (x_ss.at[3 + s], x_rs.at[3 + s]))
        moved.start()
        own = pltpu.make_async_copy(grad.at[s, me.ctx], proj_grad.at[s, mine, :], local_s.at[6 + s])
        own.start()
        return moved, own

    grads = [grad_of(0)]
    conv_backward(D, M, skip_rows, dmix)

    def dkv_step(r, c):
        at_r = pl.ds(BLK * r, BLK)
        value = dmix[at_r].astype(F32)
        for s in (1, 2):
            dshort[s, at_r] = (value * short[3 - s, at_r].astype(F32)).astype(BF)
        return c

    lax.fori_loop(0, NB // BLK, dkv_step, 0)
    grads.append(grad_of(1))
    grads.append(grad_of(2))

    filter_gradient(X, D, XR, carry, gacc, filter_grad, SCALE)
    for c in shares:
        c.wait_recv()
    for b in (0, 1):
        for k in range(4):
            cols = slice(T * k, T * k + T)
            value = share_r[b, 0, :, cols].astype(F32) + share_r[b, 1, :, cols].astype(F32)
            block_out[512 * b + T * k:512 * b + T * k + T, :] = value.T.astype(BF)
    for c in relay.sends + cots + passes + [sib] + shares:
        c.wait_send()
    for x in (proj_x, gated_x, dgated_x):
        x.all().wait_send()
    for moved, own in grads:
        own.wait()
        moved.all().wait_send()
        moved.all().wait_recv()


def write_results(block_in, grad_in, filter_in, block_out, proj_grad, filter_grad, block, grad, filters, sems):
    pieces = [(grad_in.at[n], grad.at[n], proj_grad.at[n]) for n in range(3)]
    pieces += [(block_in, block, block_out), (filter_in, filters, filter_grad)]
    reads = [pltpu.make_async_copy(a, b, sems.at[0, n]) for n, (a, b, c) in enumerate(pieces)]
    writes = [pltpu.make_async_copy(b, c, sems.at[1, n]) for n, (a, b, c) in enumerate(pieces)]
    for c in reads:
        c.start()
    for r, c in zip(reads, writes):
        r.wait()
        c.start()
    for c in writes:
        c.wait()


def local(projected, conv_weight, filters, skip_gain, out_weight, cotangent):
    dma = pltpu.SemaphoreType.DMA
    vmem = pltpu.VMEM
    blocks = vmem((NB, OWN, T), BF)
    pairs = vmem((NB, 2, OWN, T), BF)
    shares = vmem((2, 2, T, 512), BF)
    scratch = dict(
        cw=vmem((3, TAPS, C), F32), filt=vmem((G, 4096), F32), skip=vmem((1, C), F32), taps=vmem((T, T), F32),
        spread=vmem((3 * TAPS + 1, OWN, T), F32), SF=vmem((2 * T, 6 * T), BF), SB=vmem((2 * T, 6 * T), BF),
        pr=vmem((NB + 1, 3, OWN, T), BF), wg=vmem((16, C, T), BF), cotg=vmem((2, 2048, T), BF),
        short=vmem((3, NB, OWN, T), BF), mix=blocks, longm=blocks, gated_s=vmem((16, 2, OWN, T), BF), gated_r=pairs,
        gated_t=vmem((2 * T, C), BF), acc=vmem((C, 2 * T), F32), dgated_s=pairs, dgated_r=pairs, dmix=blocks,
        dshort=vmem((3, NB + 1, OWN, T), BF), grad=vmem((3, NB, OWN, T), BF), share_s=vmem((2, 2, 2, T, 512), BF),
        sib_r=shares, pre_s=shares, share_r=shares, hpad=vmem((G, 4096 + T), F32), M=vmem((G, 256, 4096 + T), BF),
        X=vmem((G, 512, 256), BF), D=vmem((G, 512, 256), BF), XR=vmem((G, 256, 256), BF), carry=vmem((G, T, T), F32),
        gacc=vmem((G, 4352), F32), local_s=dma((9,)),
        relay_ss=dma((40,)), relay_rs=dma((40,)), x_ss=dma((6,)), x_rs=dma((6,)), cot_ss=dma((3,)), cot_rs=dma((3,)),
        pass_ss=dma((4,)), pass_rs=dma((4,)), sib_ss=dma, sib_rs=dma, share_ss=dma((3,)), share_rs=dma((3,)))
    anywhere = pl.BlockSpec(memory_space=pl.ANY)
    whole = pl.BlockSpec(memory_space=pltpu.VMEM)
    block_out, proj_grad, filter_grad = pl.pallas_call(
        kernel,
        out_shape=(
            jax.ShapeDtypeStruct((C, T), BF),
            jax.ShapeDtypeStruct((3, C, T), BF),
            jax.ShapeDtypeStruct((G, 4096), F32),
        ),
        in_specs=[anywhere] * 6,
        out_specs=(whole, anywhere, whole),
        scratch_shapes=list(scratch.values()),
        compiler_params=pltpu.CompilerParams(collective_id=1, has_side_effects=True, vmem_limit_bytes=60 << 20),
        name="hyena_block",
    )(projected, conv_weight.transpose(1, 0, 2), filters[0], skip_gain[None], out_weight, cotangent)
    block_out, proj_grad, filter_grad = pl.pallas_call(
        write_results,
        out_shape=[jax.ShapeDtypeStruct(v.shape, v.dtype) for v in (block_out, proj_grad, filter_grad)],
        in_specs=[anywhere] * 3,
        out_specs=[anywhere] * 3,
        scratch_shapes=[vmem((C, T), BF), vmem((3, C, T), BF), vmem((G, 4096), F32), dma((2, 5))],
        name="write_results",
    )(block_out, proj_grad, filter_grad)
    return block_out, proj_grad, filter_grad[None]


def solution(mesh):
    return jax.shard_map(
        local,
        mesh=mesh,
        in_specs=(
            P(None, "tp", "ctx"),
            P(None, None, "tp"),
            P("tp", "ctx", None),
            P("tp"),
            P("tp", "ctx"),
            P("tp", "ctx"),
        ),
        out_specs=(P("tp", "ctx"), P(None, "tp", "ctx"), P("tp", "ctx", None)),
        check_vma=False,
    )
```

```python
import math

import jax
import jax.numpy as jnp
from jax import lax
from jax.experimental import pallas as pl
from jax.experimental.pallas import tpu as pltpu
from jax.sharding import PartitionSpec as P

BF, F32 = jnp.bfloat16, jnp.float32
MESH = pl.DeviceIdType.MESH
NB = 32
OWN = 32
G = 2
T = 128
C = 1024
TAPS = 7
SCALE = 1.0 / math.sqrt(16 * 4096)


def dot(a, b, ca, cb):
    return lax.dot_general(a, b, (((ca,), (cb,)), ((), ())), preferred_element_type=F32)


def at(value, multiple):
    return pl.multiple_of(value, multiple)


def build_toeplitz(h_ref, hpad, M):
    for g in range(G):
        hpad[g:g + 1, 0:128] = jnp.zeros((1, 128), F32)
        hpad[g:g + 1, 128:] = h_ref[g:g + 1, :]
        M[g, 128:256, 0:128] = jnp.zeros((128, 128), BF)
    def step(e, c):
        for g in range(G):
            seg = hpad[g:g + 1, pl.ds(pl.multiple_of(e * 128, 128), 256)]
            tile = pltpu.roll(jnp.broadcast_to(seg, (128, 256)), 0, 1, stride=1, stride_axis=0)[:, 128:].astype(BF)
            M[g, 0:128, pl.ds(pl.multiple_of(e * 128, 128), 128)] = tile
            M[g, 128:256, pl.ds(pl.multiple_of(e * 128 + 128, 128), 128)] = tile
        return c
    lax.fori_loop(0, NB, step, 0)


def load_pairs(own, X, row0):
    for g in range(G):
        for h in range(2):
            v = own[...].reshape(NB // 2, 2, OWN, T)[:, h, 16 * g:16 * g + 16, :]
            X[g, row0:row0 + 256, T * h:T * h + T] = v.reshape(256, T)


def store_pairs(y, out, g):
    for j in range(NB // 2):
        for h in range(2):
            out[2 * j + h, 16 * g:16 * g + 16, :] = y[16 * j:16 * j + 16, T * h:T * h + T].astype(out.dtype)


def conv_forward(X, M, skip_rows, out):
    for g in range(G):
        acc = jnp.zeros((256, 256), F32)
        for d in range(16):
            acc = acc + dot(X[g, 256 - 16 * d:512 - 16 * d, :], M[g, :, 256 * d:256 * d + 256], 1, 0)
        y = acc + skip_rows(g) * X[g, 256:512, :].astype(F32)
        store_pairs(y, out, g)


def conv_backward(D, M, skip_rows, out):
    for g in range(G):
        acc = jnp.zeros((256, 256), F32)
        for d in range(16):
            acc = acc + dot(D[g, 16 * d:16 * d + 256, :], M[g, :, 256 * d:256 * d + 256], 1, 1)
        y = acc + skip_rows(g) * D[g, 0:256, :].astype(F32)
        store_pairs(y, out, g)


def filter_gradient(X, D, XR, carry, gacc, out, scaling):
    rows = lax.broadcasted_iota(jnp.int32, (256, 256), 0)
    cols = lax.broadcasted_iota(jnp.int32, (256, 256), 1)
    flip = jnp.where(rows + cols == 255, 1.0, 0.0).astype(BF)
    for g in range(G):
        XR[g] = dot(flip, X[g, 256:512, :], 1, 1).astype(BF)
    gacc[...] = jnp.zeros(gacc.shape, F32)
    carry[...] = jnp.zeros(carry.shape, F32)
    def shear(tile):
        wide = jnp.concatenate([tile, jnp.zeros((128, 128), F32)], axis=1)
        return jnp.sum(pltpu.roll(wide, 1, 1, stride=1, stride_axis=0), axis=0, keepdims=True)
    def step(d, c):
        for g in range(G):
            p = dot(XR[g], D[g, pl.ds(pl.multiple_of(16 * d, 16), 256), :], 1, 0)
            at = pl.multiple_of(256 * d, 128)
            gacc[g:g + 1, pl.ds(at, 256)] += shear(p[0:128, 0:128] + carry[g])
            at = pl.multiple_of(256 * d + 128, 128)
            gacc[g:g + 1, pl.ds(at, 256)] += shear(p[0:128, 128:] + p[128:, 0:128])
            carry[g] = p[128:, 128:]
        return c
    lax.fori_loop(0, 16, step, 0)
    for g in range(G):
        last = shear(carry[g])
        gacc[g:g + 1, 4096:4352] += last
        out[g:g + 1, :] = gacc[g:g + 1, 256:4352] * scaling


class Place:
    def __init__(self):
        self.ctx = lax.axis_index("ctx")
        self.tp = lax.axis_index("tp")
        self.x = self.ctx // 8
        self.lo = (self.ctx // 4) % 2
        self.z = self.ctx % 4
        self.hi = self.tp // 2
        self.core = self.tp % 2
        self.partner = self.ctx + 4 - 8 * self.lo
        self.sibling = self.tp + 1 - 2 * self.core
        self.across = (self.tp + 2) % 4

    def plane(self, x, z):
        return x * 8 + self.lo * 4 + z

    def group(self):
        return [(self.ctx, self.across), (self.partner, self.tp), (self.partner, self.across)]


def barrier_signals(me):
    sem = pltpu.get_barrier_semaphore()

    def one(k, c):
        pl.semaphore_signal(sem, inc=1, device_id=((me.ctx + k) % NB, me.tp), device_id_type=MESH)
        return c

    lax.fori_loop(1, NB, one, 0)
    for dev in ((me.ctx, me.sibling), (me.ctx, me.across), (me.partner, me.across)):
        pl.semaphore_signal(sem, inc=1, device_id=dev, device_id_type=MESH)
    return sem


def remote(src, dst, ssem, rsem, dev):
    return pltpu.make_async_remote_copy(
        src_ref=src, dst_ref=dst, send_sem=ssem, recv_sem=rsem, device_id=dev, device_id_type=MESH)


class Relay:
    def __init__(self, me, w, wg, ssem, rsem):
        self.me, self.w, self.wg, self.ssem, self.rsem = me, w, wg, ssem, rsem
        self.sends = []
        self.first = [None, None]
        self.fwd = [[None, None], [None, None]]
        self.second = [{}, {}]
        self.last = [{}, {}]

    def slot(self, h, f, s):
        me = self.me
        if h == 0:
            return ((me.x + s) % 4) * 4 + (me.z + f) % 4
        return ((me.x + f) % 4) * 4 + (me.z + s) % 4

    def dev(self, h, f, s):
        me = self.me
        if h == 0:
            return me.plane((me.x + s) % 4, (me.z + f) % 4)
        return me.plane((me.x + f) % 4, (me.z + s) % 4)

    def send(self, src, dst, dev):
        n = len(self.sends)
        c = remote(src, dst, self.ssem.at[n], self.rsem.at[n], (dev, self.me.tp))
        c.start()
        self.sends.append(c)
        return c

    def part(self, b, r, n):
        return self.wg.at[b, pl.ds(r, n), :]

    def own(self, h):
        return self.w.at[pl.ds(512 * h, 512), :]

    def pair(self, h, f):
        b = self.slot(h, f, 0)
        dst = self.part(b, 512 * h, 512)
        src = self.own(h) if f == 0 else dst
        self.second[h][f] = [self.send(src, dst, self.dev(h, 0, 1)), self.send(src, dst, self.dev(h, 0, -1))]

    def begin(self):
        for h in (0, 1):
            dst = self.part(self.slot(h, 0, 0), 512 * h, 512)
            self.first[h] = [self.send(self.own(h), dst, self.dev(h, 1, 0)), self.send(self.own(h), dst, self.dev(h, -1, 0))]

    def neighbours(self):
        for i, f in ((0, -1), (1, 1)):
            for h in (0, 1):
                self.first[h][i].wait_recv()
                part = self.part(self.slot(h, f, 0), 512 * h + 256 * i, 256)
                self.fwd[h][i] = self.send(part, part, self.dev(h, -f, 0))
                self.pair(h, f)

    def opposite(self):
        for h in (0, 1):
            for i in (0, 1):
                self.fwd[h][i].wait_recv()
            self.pair(h, 2)

    def forward(self, h, f):
        cs = []
        for i, s in ((0, -1), (1, 1)):
            self.second[h][f][i].wait_recv()
            part = self.part(self.slot(h, f, s), 512 * h + 256 * i, 256)
            cs.append(self.send(part, part, self.dev(h, 0, -s)))
        self.last[h][f] = cs

    def finish(self, h, f):
        for c in self.last[h][f]:
            c.wait_recv()


class Exchange:
    def __init__(self, me, src, dst, whole, sems):
        self.me, self.src, self.dst, self.whole, self.sems = me, src, dst, whole, sems

    def start(self):
        def go(k, c):
            to = (self.me.ctx + k) % NB
            remote(self.src(to), self.dst, self.sems[0], self.sems[1], (to, self.me.tp)).start()
            return c

        lax.fori_loop(1, NB, go, 0)

    def start_half(self, h):
        def go(k, c):
            to = 16 * h + (self.me.ctx + k) % 16
            remote(self.src(to), self.dst, self.sems[0], self.sems[1], (to, self.me.tp)).start()
            return c

        lax.fori_loop(1 - (self.me.ctx // 16 + h) % 2, 16, go, 0)

    def all(self):
        return remote(self.whole, self.whole, self.sems[0], self.sems[1], (self.me.partner, self.me.tp))


def lanes(shape):
    return lax.broadcasted_iota(jnp.int32, shape, len(shape) - 1)


def shift_matrix(SH, backward):
    for j in range(1, TAPS):
        rows = lax.broadcasted_iota(jnp.int32, (2 * T, T), 0)
        col = lanes((2 * T, T))
        source = col + j if backward else (col + (2 * T - j)) % (2 * T)
        SH[:, T * (j - 1):T * j] = jnp.where(rows == source, 1.0, 0.0).astype(BF)


def own_taps(me, cw, skip, taps, spread):
    at_block = pl.ds(at((me.ctx // 4) * T, T), T)
    rows = [cw[s, j:j + 1, at_block] for j in range(TAPS) for s in range(3)] + [skip[:, at_block]]
    rows = jnp.concatenate(rows + [jnp.zeros((T - len(rows), T), F32)], axis=0)
    taps[...] = rows.T
    own = taps[pl.ds(at((me.ctx % 4) * OWN, OWN), OWN), :]
    for n in range(3 * TAPS + 1):
        spread[n] = jnp.broadcast_to(own[:, n:n + 1], (OWN, T))


def short_conv(s, x, beside, SH, spread, blocks):
    both = jnp.concatenate([x, beside], axis=1)
    total = x.reshape(blocks, OWN, T).astype(F32) * spread[s][None]
    for p in range(3):
        moved = dot(both, SH[:, 2 * T * p:2 * T * p + 2 * T], 1, 0)
        for i in (0, 1):
            j = 2 * p + i + 1
            total = total + moved[:, T * i:T * i + T].reshape(blocks, OWN, T) * spread[3 * j + s][None]
    return total


def kernel(proj, cw_in, filt_in, skip_in, w, cot, block_out, proj_grad, filter_grad,
           cw, filt, skip, taps, spread, SF, SB, pr, wg, cotg, short, mix, longm, gated_s, gated_r, gated_t, acc,
           dgated_s, dgated_r, dmix, dshort, grad, share_s, sib_r, pre_s, share_r, hpad, M, X, D, XR, carry, gacc,
           local_s, relay_ss, relay_rs, x_ss, x_rs, cot_ss, cot_rs, pass_ss, pass_rs, sib_ss, sib_rs, share_ss, share_rs):
    me = Place()
    sem = barrier_signals(me)
    BLK = 8
    mine = pl.ds(at(OWN * me.ctx, OWN), OWN)
    half = pl.ds(at(512 * me.tp, 512), 512)

    def class_rows(lo):
        return cot.at[pl.ds(at(512 * lo, 512), 512), :]

    loads = [(cw_in, cw), (filt_in, filt), (skip_in, skip), (w, wg.at[me.x * 4 + me.z]),
             (class_rows(me.lo), cotg.at[me.lo, half, :]), (proj.at[:, mine, :], pr.at[me.ctx + 1])]
    loads = [pltpu.make_async_copy(a, b, local_s.at[n]) for n, (a, b) in enumerate(loads)]
    for c in loads:
        c.start()
    shift_matrix(SF, False)
    shift_matrix(SB, True)
    pr[0] = jnp.zeros((3, OWN, T), BF)
    for s in range(3):
        dshort[s, NB] = jnp.zeros((OWN, T), BF)
    X[:, 0:256, :] = jnp.zeros((G, 256, 256), BF)
    D[:, 256:512, :] = jnp.zeros((G, 256, 256), BF)
    pl.semaphore_wait(sem, NB - 1 + 3)

    relay = Relay(me, w, wg, relay_ss, relay_rs)
    relay.begin()
    cots = []
    for n, (ctx, tp) in enumerate(me.group()):
        lo = me.lo if n == 0 else 1 - me.lo
        cots.append(remote(class_rows(lo), cotg.at[me.lo, half, :], cot_ss.at[n], cot_rs.at[n], (ctx, tp)))
        cots[n].start()
    passes = [remote(class_rows(me.lo), cotg.at[me.lo, half, :], pass_ss.at[3], pass_rs.at[3], (me.ctx, me.sibling))]
    passes[0].start()
    for h in (0, 1):
        relay.pair(h, 0)
    def skip_rows(g):
        s = spread[3 * TAPS][16 * g:16 * g + 16, :]
        s = jnp.concatenate([s, s], axis=1)
        return jnp.broadcast_to(s[None], (16, 16, 256)).reshape(256, 256)

    def slots(h, f):
        if h == 0:
            return [k * 4 + (me.z + f) % 4 for k in range(4)]
        return [((me.x + f) % 4) * 4 + k for k in range(4)]

    def product(h, f, r, right):
        left = jnp.concatenate([wg[s, r:r + 256, :] for s in slots(h, f)], axis=1)
        return dot(left, right, 1, 0)

    def columns(h, f):
        return jnp.concatenate([
            jnp.concatenate([cotg[b, pl.ds(at(s * T, T), T), :] for s in slots(h, f)], axis=0) for b in (0, 1)], axis=1)

    dgated_x = Exchange(me, lambda to: dgated_s.at[to], dgated_r.at[me.ctx], dgated_r.at[pl.ds(0, NB - 1)],
                        (x_ss.at[2], x_rs.at[2]))

    def contract(f):
        for h in (0, 1):
            relay.finish(h, f)
            right = columns(h, f)
            for r in (512 * h, 512 * h + 256):
                value = product(h, f, r, right)
                if f != 0:
                    value = value + acc[r:r + 256, :]
                if f != 2:
                    acc[r:r + 256, :] = value
                    continue
                for b in (0, 1):
                    dgated_s[r // OWN:r // OWN + 8, b] = value[:, T * b:T * b + T].astype(BF).reshape(8, OWN, T)
            if f == 2:
                dgated_x.start_half(h)

    proj_x = Exchange(me, lambda to: proj.at[:, pl.ds(at(OWN * to, OWN), OWN), :], pr.at[me.ctx + 1],
                      pr.at[pl.ds(1, NB - 1)], (x_ss.at[0], x_rs.at[0]))
    proj_x.start()
    for c in loads[:3]:
        c.wait()
    own_taps(me, cw, skip, taps, spread)
    relay.neighbours()
    build_toeplitz(filt, hpad, M)
    for h in (0, 1):
        relay.forward(h, 0)
    relay.opposite()
    for c in loads[3:]:
        c.wait()
    proj_x.all().wait_recv()

    def short_step(r, c):
        outs = []
        for s in range(3):
            x = pr[pl.ds(BLK * r + 1, BLK), s].reshape(BLK * OWN, T)
            before = pr[pl.ds(BLK * r, BLK), s].reshape(BLK * OWN, T)
            out = short_conv(s, x, before, SF, spread, BLK).astype(BF)
            short[s, pl.ds(BLK * r, BLK)] = out
            outs.append(out.astype(F32))
        mix[pl.ds(BLK * r, BLK)] = (outs[1] * outs[2]).astype(BF)
        return c

    lax.fori_loop(0, NB // BLK, short_step, 0)
    across = pl.ds(at(512 * me.across, 512), 512)
    came = [(me.lo, across), (1 - me.lo, half), (1 - me.lo, across)]
    for n, (lo, rows) in enumerate(came):
        cots[n].wait_recv()
        part = cotg.at[lo, rows, :]
        c = remote(part, part, pass_ss.at[n], pass_rs.at[n], (me.ctx, me.sibling))
        c.start()
        passes.append(c)
    for h in (0, 1):
        relay.forward(h, -1)
    load_pairs(mix, X, 256)
    conv_forward(X, M, skip_rows, longm)
    for x in range(4):
        for b in (0, 1):
            for z in range(4):
                n = 8 * x + 4 * b + z
                gated_s[4 * x + z, b] = (short[0, n].astype(F32) * longm[n].astype(F32)).astype(BF)
    for h in (0, 1):
        relay.forward(h, 1)
    gated_x = Exchange(me, lambda to: gated_s.at[(to // 8) * 4 + to % 4], gated_r.at[me.ctx],
                       gated_r.at[pl.ds(0, NB - 1)], (x_ss.at[1], x_rs.at[1]))
    gated_x.start()
    gated_r[me.ctx] = gated_s[me.x * 4 + me.z]
    for c in passes:
        c.wait_recv()
    contract(0)
    for h in (0, 1):
        relay.forward(h, 2)
    contract(-1)
    contract(1)
    contract(2)
    dgated_r[me.ctx] = dgated_s[me.ctx]

    gated_x.all().wait_recv()
    for b in (0, 1):
        for k in range(C // T):
            block = gated_r[4 * k:4 * k + 4, b].reshape(T, T).astype(F32)
            gated_t[T * b:T * b + T, T * k:T * k + T] = block.T.astype(BF)
    sib = remote(share_s.at[0], sib_r, sib_ss, sib_rs, (me.ctx, me.sibling))
    for mine_too in (0, 1):
        parity = me.core if mine_too else 1 - me.core
        for hi in (0, 1):
            x = 2 * hi + parity
            for p in (0, 1):
                right = jnp.concatenate([wg[4 * x + 2 * p], wg[4 * x + 2 * p + 1]], axis=1)
                value = dot(gated_t[...], right, 1, 0).astype(BF)
                for b in (0, 1):
                    share_s[mine_too, b, hi, :, 256 * p:256 * p + 256] = value[T * b:T * b + T, :]
        if not mine_too:
            sib.start()
    sib.wait_recv()
    for b in (0, 1):
        for hi in (0, 1):
            value = share_s[1, b, hi].astype(F32) + sib_r[b, hi].astype(F32)
            pre_s[b, hi] = value.astype(BF)
    shares = []
    for n, (ctx, tp) in enumerate(me.group()):
        b = me.lo if n == 0 else 1 - me.lo
        hi = me.hi if n == 1 else 1 - me.hi
        shares.append(remote(pre_s.at[b, hi], share_r.at[me.lo, me.hi], share_ss.at[n], share_rs.at[n], (ctx, tp)))
        shares[n].start()
    share_r[me.lo, me.hi] = pre_s[me.lo, me.hi]

    dgated_x.all().wait_recv()
    for n in range(NB):
        b, pair = (n // 4) % 2, n - n % 8 + n % 4
        value = (dgated_r[pair, b].astype(F32) + dgated_r[pair + 4, b].astype(F32)).astype(BF).astype(F32)
        dlong = (value * short[0, n].astype(F32)).astype(BF)
        for g in range(G):
            row = 16 * (n // 2)
            D[g, row:row + 16, T * (n % 2):T * (n % 2) + T] = dlong[16 * g:16 * g + 16, :]
        dshort[0, n] = (value * longm[n].astype(F32)).astype(BF)

    def grad_of(streams, n):
        def step(r, c):
            for s in streams:
                x = dshort[s, pl.ds(BLK * r, BLK)].reshape(BLK * OWN, T)
                after = dshort[s, pl.ds(BLK * r + 1, BLK)].reshape(BLK * OWN, T)
                grad[pl.ds(BLK * r, BLK), s] = short_conv(s, x, after, SB, spread, BLK).astype(BF)
            return c

        lax.fori_loop(0, NB // BLK, step, 0)
        some = pl.ds(streams[0], len(streams))
        moved = Exchange(me, lambda to: grad.at[to, some], proj_grad.at[some, mine, :],
                         proj_grad.at[some, pl.ds(0, C - OWN), :], (x_ss.at[3 + n], x_rs.at[3 + n]))
        moved.start()
        own = pltpu.make_async_copy(grad.at[me.ctx, some], proj_grad.at[some, mine, :], local_s.at[6 + n])
        own.start()
        return moved, own

    grads = [grad_of((0,), 0)]
    conv_backward(D, M, skip_rows, dmix)

    def dkv_step(r, c):
        at_r = pl.ds(BLK * r, BLK)
        value = dmix[at_r].astype(F32)
        for s in (1, 2):
            dshort[s, at_r] = (value * short[3 - s, at_r].astype(F32)).astype(BF)
        return c

    lax.fori_loop(0, NB // BLK, dkv_step, 0)
    grads.append(grad_of((1, 2), 1))

    filter_gradient(X, D, XR, carry, gacc, filter_grad, SCALE)
    for c in shares:
        c.wait_recv()
    for b in (0, 1):
        for k in range(4):
            cols = slice(T * k, T * k + T)
            value = share_r[b, 0, :, cols].astype(F32) + share_r[b, 1, :, cols].astype(F32)
            block_out[512 * b + T * k:512 * b + T * k + T, :] = value.T.astype(BF)
    for c in relay.sends + cots + passes + [sib] + shares:
        c.wait_send()
    for x in (proj_x, gated_x, dgated_x):
        x.all().wait_send()
    for moved, own in grads:
        own.wait()
        moved.all().wait_send()
        moved.all().wait_recv()


def write_results(block_in, grad_in, filter_in, block_out, proj_grad, filter_grad, block, grad, filters, sems):
    cuts = [pl.ds(256 * n, 256) for n in range(4)]
    pieces = [(grad_in.at[n, c], grad.at[n, c], proj_grad.at[n, c]) for n in range(3) for c in cuts]
    pieces += [(block_in.at[c], block.at[c], block_out.at[c]) for c in cuts] + [(filter_in, filters, filter_grad)]
    reads = [pltpu.make_async_copy(a, b, sems.at[0, n]) for n, (a, b, c) in enumerate(pieces)]
    writes = [pltpu.make_async_copy(b, c, sems.at[1, n]) for n, (a, b, c) in enumerate(pieces)]
    for c in reads:
        c.start()
    for r, c in zip(reads, writes):
        r.wait()
        c.start()
    for c in writes:
        c.wait()


def local(projected, conv_weight, filters, skip_gain, out_weight, cotangent):
    dma = pltpu.SemaphoreType.DMA
    vmem = pltpu.VMEM
    blocks = vmem((NB, OWN, T), BF)
    pairs = vmem((NB, 2, OWN, T), BF)
    shares = vmem((2, 2, T, 512), BF)
    scratch = dict(
        cw=vmem((3, TAPS, C), F32), filt=vmem((G, 4096), F32), skip=vmem((1, C), F32), taps=vmem((T, T), F32),
        spread=vmem((3 * TAPS + 1, OWN, T), F32), SF=vmem((2 * T, 6 * T), BF), SB=vmem((2 * T, 6 * T), BF),
        pr=vmem((NB + 1, 3, OWN, T), BF), wg=vmem((16, C, T), BF), cotg=vmem((2, 2048, T), BF),
        short=vmem((3, NB, OWN, T), BF), mix=blocks, longm=blocks, gated_s=vmem((16, 2, OWN, T), BF), gated_r=pairs,
        gated_t=vmem((2 * T, C), BF), acc=vmem((C, 2 * T), F32), dgated_s=pairs, dgated_r=pairs, dmix=blocks,
        dshort=vmem((3, NB + 1, OWN, T), BF), grad=vmem((NB, 3, OWN, T), BF), share_s=vmem((2, 2, 2, T, 512), BF),
        sib_r=shares, pre_s=shares, share_r=shares, hpad=vmem((G, 4096 + T), F32), M=vmem((G, 256, 4096 + T), BF),
        X=vmem((G, 512, 256), BF), D=vmem((G, 512, 256), BF), XR=vmem((G, 256, 256), BF), carry=vmem((G, T, T), F32),
        gacc=vmem((G, 4352), F32), local_s=dma((9,)),
        relay_ss=dma((40,)), relay_rs=dma((40,)), x_ss=dma((6,)), x_rs=dma((6,)), cot_ss=dma((3,)), cot_rs=dma((3,)),
        pass_ss=dma((4,)), pass_rs=dma((4,)), sib_ss=dma, sib_rs=dma, share_ss=dma((3,)), share_rs=dma((3,)))
    anywhere = pl.BlockSpec(memory_space=pl.ANY)
    whole = pl.BlockSpec(memory_space=pltpu.VMEM)
    block_out, proj_grad, filter_grad = pl.pallas_call(
        kernel,
        out_shape=(
            jax.ShapeDtypeStruct((C, T), BF),
            jax.ShapeDtypeStruct((3, C, T), BF),
            jax.ShapeDtypeStruct((G, 4096), F32),
        ),
        in_specs=[anywhere] * 6,
        out_specs=(whole, anywhere, whole),
        scratch_shapes=list(scratch.values()),
        compiler_params=pltpu.CompilerParams(collective_id=1, has_side_effects=True, vmem_limit_bytes=60 << 20),
        name="hyena_block",
    )(projected, conv_weight.transpose(1, 0, 2), filters[0], skip_gain[None], out_weight, cotangent)
    block_out, proj_grad, filter_grad = pl.pallas_call(
        write_results,
        out_shape=[jax.ShapeDtypeStruct(v.shape, v.dtype) for v in (block_out, proj_grad, filter_grad)],
        in_specs=[anywhere] * 3,
        out_specs=[anywhere] * 3,
        scratch_shapes=[vmem((C, T), BF), vmem((3, C, T), BF), vmem((G, 4096), F32), dma((2, 17))],
        name="write_results",
    )(block_out, proj_grad, filter_grad)
    return block_out, proj_grad, filter_grad[None]


def solution(mesh):
    return jax.shard_map(
        local,
        mesh=mesh,
        in_specs=(
            P(None, "tp", "ctx"),
            P(None, None, "tp"),
            P("tp", "ctx", None),
            P("tp"),
            P("tp", "ctx"),
            P("tp", "ctx"),
        ),
        out_specs=(P("tp", "ctx"), P(None, "tp", "ctx"), P("tp", "ctx", None)),
        check_vma=False,
    )
```

```python
import math

import jax
import jax.numpy as jnp
from jax import lax
from jax.experimental import pallas as pl
from jax.experimental.pallas import tpu as pltpu
from jax.sharding import PartitionSpec as P

BF, F32 = jnp.bfloat16, jnp.float32
MESH = pl.DeviceIdType.MESH
NB = 32
OWN = 32
G = 2
T = 128
C = 1024
TAPS = 7
SCALE = 1.0 / math.sqrt(16 * 4096)


def dot(a, b, ca, cb):
    return lax.dot_general(a, b, (((ca,), (cb,)), ((), ())), preferred_element_type=F32)


def at(value, multiple):
    return pl.multiple_of(value, multiple)


def build_toeplitz(h_ref, hpad, M):
    for g in range(G):
        hpad[g:g + 1, 0:128] = jnp.zeros((1, 128), F32)
        hpad[g:g + 1, 128:] = h_ref[g:g + 1, :]
        M[g, 128:256, 0:128] = jnp.zeros((128, 128), BF)
    def step(e, c):
        for g in range(G):
            seg = hpad[g:g + 1, pl.ds(pl.multiple_of(e * 128, 128), 256)]
            tile = pltpu.roll(jnp.broadcast_to(seg, (128, 256)), 0, 1, stride=1, stride_axis=0)[:, 128:].astype(BF)
            M[g, 0:128, pl.ds(pl.multiple_of(e * 128, 128), 128)] = tile
            M[g, 128:256, pl.ds(pl.multiple_of(e * 128 + 128, 128), 128)] = tile
        return c
    lax.fori_loop(0, NB, step, 0)


def load_pairs(own, X, row0):
    for g in range(G):
        for h in range(2):
            v = own[...].reshape(NB // 2, 2, OWN, T)[:, h, 16 * g:16 * g + 16, :]
            X[g, row0:row0 + 256, T * h:T * h + T] = v.reshape(256, T)


def store_pairs(y, out, g):
    for j in range(NB // 2):
        for h in range(2):
            out[2 * j + h, 16 * g:16 * g + 16, :] = y[16 * j:16 * j + 16, T * h:T * h + T].astype(out.dtype)


def conv_forward(X, M, skip_rows, out):
    for g in range(G):
        acc = jnp.zeros((256, 256), F32)
        for d in range(16):
            acc = acc + dot(X[g, 256 - 16 * d:512 - 16 * d, :], M[g, :, 256 * d:256 * d + 256], 1, 0)
        y = acc + skip_rows(g) * X[g, 256:512, :].astype(F32)
        store_pairs(y, out, g)


def conv_backward(D, M, skip_rows, out):
    for g in range(G):
        acc = jnp.zeros((256, 256), F32)
        for d in range(16):
            acc = acc + dot(D[g, 16 * d:16 * d + 256, :], M[g, :, 256 * d:256 * d + 256], 1, 1)
        y = acc + skip_rows(g) * D[g, 0:256, :].astype(F32)
        store_pairs(y, out, g)


def filter_gradient(X, D, XR, carry, gacc, out, scaling):
    rows = lax.broadcasted_iota(jnp.int32, (256, 256), 0)
    cols = lax.broadcasted_iota(jnp.int32, (256, 256), 1)
    flip = jnp.where(rows + cols == 255, 1.0, 0.0).astype(BF)
    for g in range(G):
        XR[g] = dot(flip, X[g, 256:512, :], 1, 1).astype(BF)
    gacc[...] = jnp.zeros(gacc.shape, F32)
    carry[...] = jnp.zeros(carry.shape, F32)
    def shear(tile):
        wide = jnp.concatenate([tile, jnp.zeros((128, 128), F32)], axis=1)
        return jnp.sum(pltpu.roll(wide, 1, 1, stride=1, stride_axis=0), axis=0, keepdims=True)
    def step(d, c):
        for g in range(G):
            p = dot(XR[g], D[g, pl.ds(pl.multiple_of(16 * d, 16), 256), :], 1, 0)
            at = pl.multiple_of(256 * d, 128)
            gacc[g:g + 1, pl.ds(at, 256)] += shear(p[0:128, 0:128] + carry[g])
            at = pl.multiple_of(256 * d + 128, 128)
            gacc[g:g + 1, pl.ds(at, 256)] += shear(p[0:128, 128:] + p[128:, 0:128])
            carry[g] = p[128:, 128:]
        return c
    lax.fori_loop(0, 16, step, 0)
    for g in range(G):
        last = shear(carry[g])
        gacc[g:g + 1, 4096:4352] += last
        out[g:g + 1, :] = gacc[g:g + 1, 256:4352] * scaling


class Place:
    def __init__(self):
        self.ctx = lax.axis_index("ctx")
        self.tp = lax.axis_index("tp")
        self.x = self.ctx // 8
        self.lo = (self.ctx // 4) % 2
        self.z = self.ctx % 4
        self.hi = self.tp // 2
        self.core = self.tp % 2
        self.partner = self.ctx + 4 - 8 * self.lo
        self.sibling = self.tp + 1 - 2 * self.core
        self.across = (self.tp + 2) % 4

    def plane(self, x, z):
        return x * 8 + self.lo * 4 + z

    def group(self):
        return [(self.ctx, self.across), (self.partner, self.tp), (self.partner, self.across)]


def barrier_signals(me):
    sem = pltpu.get_barrier_semaphore()

    def one(k, c):
        pl.semaphore_signal(sem, inc=1, device_id=((me.ctx + k) % NB, me.tp), device_id_type=MESH)
        return c

    lax.fori_loop(1, NB, one, 0)
    for dev in ((me.ctx, me.sibling), (me.ctx, me.across), (me.partner, me.across)):
        pl.semaphore_signal(sem, inc=1, device_id=dev, device_id_type=MESH)
    return sem


def remote(src, dst, ssem, rsem, dev):
    return pltpu.make_async_remote_copy(
        src_ref=src, dst_ref=dst, send_sem=ssem, recv_sem=rsem, device_id=dev, device_id_type=MESH)


class Relay:
    def __init__(self, me, w, wg, ssem, rsem):
        self.me, self.w, self.wg, self.ssem, self.rsem = me, w, wg, ssem, rsem
        self.sends = []
        self.first = [None, None]
        self.fwd = [[None, None], [None, None]]
        self.second = [{}, {}]
        self.last = [{}, {}]

    def slot(self, h, f, s):
        me = self.me
        if h == 0:
            return ((me.x + s) % 4) * 4 + (me.z + f) % 4
        return ((me.x + f) % 4) * 4 + (me.z + s) % 4

    def dev(self, h, f, s):
        me = self.me
        if h == 0:
            return me.plane((me.x + s) % 4, (me.z + f) % 4)
        return me.plane((me.x + f) % 4, (me.z + s) % 4)

    def send(self, src, dst, dev):
        n = len(self.sends)
        c = remote(src, dst, self.ssem.at[n], self.rsem.at[n], (dev, self.me.tp))
        c.start()
        self.sends.append(c)
        return c

    def part(self, b, r, n):
        return self.wg.at[b, pl.ds(r, n), :]

    def own(self, h):
        return self.w.at[pl.ds(512 * h, 512), :]

    def pair(self, h, f):
        b = self.slot(h, f, 0)
        dst = self.part(b, 512 * h, 512)
        src = self.own(h) if f == 0 else dst
        self.second[h][f] = [self.send(src, dst, self.dev(h, 0, 1)), self.send(src, dst, self.dev(h, 0, -1))]

    def begin(self):
        for h in (0, 1):
            dst = self.part(self.slot(h, 0, 0), 512 * h, 512)
            self.first[h] = [self.send(self.own(h), dst, self.dev(h, 1, 0)), self.send(self.own(h), dst, self.dev(h, -1, 0))]

    def neighbours(self):
        for i, f in ((0, -1), (1, 1)):
            for h in (0, 1):
                self.first[h][i].wait_recv()
                part = self.part(self.slot(h, f, 0), 512 * h + 256 * i, 256)
                self.fwd[h][i] = self.send(part, part, self.dev(h, -f, 0))
                self.pair(h, f)

    def opposite(self):
        for h in (0, 1):
            for i in (0, 1):
                self.fwd[h][i].wait_recv()
            self.pair(h, 2)

    def forward(self, h, f):
        cs = []
        for i, s in ((0, -1), (1, 1)):
            self.second[h][f][i].wait_recv()
            part = self.part(self.slot(h, f, s), 512 * h + 256 * i, 256)
            cs.append(self.send(part, part, self.dev(h, 0, -s)))
        self.last[h][f] = cs

    def finish(self, h, f):
        for c in self.last[h][f]:
            c.wait_recv()


class Exchange:
    def __init__(self, me, src, dst, whole, sems):
        self.me, self.src, self.dst, self.whole, self.sems = me, src, dst, whole, sems

    def start(self):
        def go(k, c):
            to = (self.me.ctx + k) % NB
            remote(self.src(to), self.dst, self.sems[0], self.sems[1], (to, self.me.tp)).start()
            return c

        lax.fori_loop(1, NB, go, 0)

    def start_half(self, h):
        def go(k, c):
            to = 16 * h + (self.me.ctx + k) % 16
            remote(self.src(to), self.dst, self.sems[0], self.sems[1], (to, self.me.tp)).start()
            return c

        lax.fori_loop(1 - (self.me.ctx // 16 + h) % 2, 16, go, 0)

    def all(self):
        return remote(self.whole, self.whole, self.sems[0], self.sems[1], (self.me.partner, self.me.tp))


def lanes(shape):
    return lax.broadcasted_iota(jnp.int32, shape, len(shape) - 1)


def shift_matrix(SH, backward):
    for j in range(1, TAPS):
        rows = lax.broadcasted_iota(jnp.int32, (2 * T, T), 0)
        col = lanes((2 * T, T))
        source = col + j if backward else (col + (2 * T - j)) % (2 * T)
        SH[:, T * (j - 1):T * j] = jnp.where(rows == source, 1.0, 0.0).astype(BF)


def own_taps(me, cw, skip, taps, spread):
    at_block = pl.ds(at((me.ctx // 4) * T, T), T)
    rows = [cw[s, j:j + 1, at_block] for j in range(TAPS) for s in range(3)] + [skip[:, at_block]]
    rows = jnp.concatenate(rows + [jnp.zeros((T - len(rows), T), F32)], axis=0)
    taps[...] = rows.T
    own = taps[pl.ds(at((me.ctx % 4) * OWN, OWN), OWN), :]
    for n in range(3 * TAPS + 1):
        spread[n] = jnp.broadcast_to(own[:, n:n + 1], (OWN, T))


def short_conv(s, x, beside, SH, spread, blocks):
    both = jnp.concatenate([x, beside], axis=1)
    total = x.reshape(blocks, OWN, T).astype(F32) * spread[s][None]
    for p in range(3):
        moved = dot(both, SH[:, 2 * T * p:2 * T * p + 2 * T], 1, 0)
        for i in (0, 1):
            j = 2 * p + i + 1
            total = total + moved[:, T * i:T * i + T].reshape(blocks, OWN, T) * spread[3 * j + s][None]
    return total


def kernel(proj, cw_in, filt_in, skip_in, w, cot, block_out, proj_grad, filter_grad,
           cw, filt, skip, taps, spread, SF, SB, pr, pv, wg, cotg, short, mix, longm, gated_s, gated_r, gated_t, acc,
           dgated_s, dgated_r, dmix, dshort, grad, share_s, sib_r, pre_s, share_r, hpad, M, X, D, XR, carry, gacc,
           local_s, relay_ss, relay_rs, x_ss, x_rs, cot_ss, cot_rs, pass_ss, pass_rs, sib_ss, sib_rs, share_ss, share_rs):
    me = Place()
    sem = barrier_signals(me)
    BLK = 8
    mine = pl.ds(at(OWN * me.ctx, OWN), OWN)
    half = pl.ds(at(512 * me.tp, 512), 512)

    def class_rows(lo):
        return cot.at[pl.ds(at(512 * lo, 512), 512), :]

    loads = [(cw_in, cw), (filt_in, filt), (skip_in, skip), (w, wg.at[me.x * 4 + me.z]),
             (class_rows(me.lo), cotg.at[me.lo, half, :]), (proj.at[:, mine, :], pr.at[me.ctx + 1]), (proj, pv)]
    loads = [pltpu.make_async_copy(a, b, local_s.at[n]) for n, (a, b) in enumerate(loads)]
    for c in loads:
        c.start()
    shift_matrix(SF, False)
    shift_matrix(SB, True)
    pr[0] = jnp.zeros((3, OWN, T), BF)
    for s in range(3):
        dshort[s, NB] = jnp.zeros((OWN, T), BF)
    X[:, 0:256, :] = jnp.zeros((G, 256, 256), BF)
    D[:, 256:512, :] = jnp.zeros((G, 256, 256), BF)
    pl.semaphore_wait(sem, NB - 1 + 3)

    loads[3].wait()
    loads[6].wait()
    relay = Relay(me, wg.at[me.x * 4 + me.z], wg, relay_ss, relay_rs)
    relay.begin()
    cots = []
    for n, (ctx, tp) in enumerate(me.group()):
        lo = me.lo if n == 0 else 1 - me.lo
        cots.append(remote(class_rows(lo), cotg.at[me.lo, half, :], cot_ss.at[n], cot_rs.at[n], (ctx, tp)))
        cots[n].start()
    passes = [remote(class_rows(me.lo), cotg.at[me.lo, half, :], pass_ss.at[3], pass_rs.at[3], (me.ctx, me.sibling))]
    passes[0].start()
    for h in (0, 1):
        relay.pair(h, 0)
    def skip_rows(g):
        s = spread[3 * TAPS][16 * g:16 * g + 16, :]
        s = jnp.concatenate([s, s], axis=1)
        return jnp.broadcast_to(s[None], (16, 16, 256)).reshape(256, 256)

    def slots(h, f):
        if h == 0:
            return [k * 4 + (me.z + f) % 4 for k in range(4)]
        return [((me.x + f) % 4) * 4 + k for k in range(4)]

    def product(h, f, r, right):
        left = jnp.concatenate([wg[s, r:r + 256, :] for s in slots(h, f)], axis=1)
        return dot(left, right, 1, 0)

    def columns(h, f):
        return jnp.concatenate([
            jnp.concatenate([cotg[b, pl.ds(at(s * T, T), T), :] for s in slots(h, f)], axis=0) for b in (0, 1)], axis=1)

    dgated_x = Exchange(me, lambda to: dgated_s.at[to], dgated_r.at[me.ctx], dgated_r.at[pl.ds(0, NB - 1)],
                        (x_ss.at[2], x_rs.at[2]))

    def contract(f):
        for h in (0, 1):
            relay.finish(h, f)
            right = columns(h, f)
            for r in (512 * h, 512 * h + 256):
                value = product(h, f, r, right)
                if f != 0:
                    value = value + acc[r:r + 256, :]
                if f != 2:
                    acc[r:r + 256, :] = value
                    continue
                for b in (0, 1):
                    dgated_s[r // OWN:r // OWN + 8, b] = value[:, T * b:T * b + T].astype(BF).reshape(8, OWN, T)
            if f == 2:
                dgated_x.start_half(h)

    proj_x = Exchange(me, lambda to: pv.at[:, pl.ds(at(OWN * to, OWN), OWN), :], pr.at[me.ctx + 1],
                      pr.at[pl.ds(1, NB - 1)], (x_ss.at[0], x_rs.at[0]))
    proj_x.start()
    for c in loads[:3]:
        c.wait()
    own_taps(me, cw, skip, taps, spread)
    relay.neighbours()
    build_toeplitz(filt, hpad, M)
    for h in (0, 1):
        relay.forward(h, 0)
    relay.opposite()
    for c in loads[4:6]:
        c.wait()
    proj_x.all().wait_recv()

    def short_step(r, c):
        outs = []
        for s in range(3):
            x = pr[pl.ds(BLK * r + 1, BLK), s].reshape(BLK * OWN, T)
            before = pr[pl.ds(BLK * r, BLK), s].reshape(BLK * OWN, T)
            out = short_conv(s, x, before, SF, spread, BLK).astype(BF)
            short[s, pl.ds(BLK * r, BLK)] = out
            outs.append(out.astype(F32))
        mix[pl.ds(BLK * r, BLK)] = (outs[1] * outs[2]).astype(BF)
        return c

    lax.fori_loop(0, NB // BLK, short_step, 0)
    across = pl.ds(at(512 * me.across, 512), 512)
    came = [(me.lo, across), (1 - me.lo, half), (1 - me.lo, across)]
    for n, (lo, rows) in enumerate(came):
        cots[n].wait_recv()
        part = cotg.at[lo, rows, :]
        c = remote(part, part, pass_ss.at[n], pass_rs.at[n], (me.ctx, me.sibling))
        c.start()
        passes.append(c)
    for h in (0, 1):
        relay.forward(h, -1)
    load_pairs(mix, X, 256)
    conv_forward(X, M, skip_rows, longm)
    for x in range(4):
        for b in (0, 1):
            for z in range(4):
                n = 8 * x + 4 * b + z
                gated_s[4 * x + z, b] = (short[0, n].astype(F32) * longm[n].astype(F32)).astype(BF)
    for h in (0, 1):
        relay.forward(h, 1)
    gated_x = Exchange(me, lambda to: gated_s.at[(to // 8) * 4 + to % 4], gated_r.at[me.ctx],
                       gated_r.at[pl.ds(0, NB - 1)], (x_ss.at[1], x_rs.at[1]))
    gated_x.start()
    gated_r[me.ctx] = gated_s[me.x * 4 + me.z]
    for c in passes:
        c.wait_recv()
    contract(0)
    for h in (0, 1):
        relay.forward(h, 2)
    contract(-1)
    contract(1)
    contract(2)
    dgated_r[me.ctx] = dgated_s[me.ctx]

    gated_x.all().wait_recv()
    for b in (0, 1):
        for k in range(C // T):
            block = gated_r[4 * k:4 * k + 4, b].reshape(T, T).astype(F32)
            gated_t[T * b:T * b + T, T * k:T * k + T] = block.T.astype(BF)
    sib = remote(share_s.at[0], sib_r, sib_ss, sib_rs, (me.ctx, me.sibling))
    for mine_too in (0, 1):
        parity = me.core if mine_too else 1 - me.core
        for hi in (0, 1):
            x = 2 * hi + parity
            for p in (0, 1):
                right = jnp.concatenate([wg[4 * x + 2 * p], wg[4 * x + 2 * p + 1]], axis=1)
                value = dot(gated_t[...], right, 1, 0).astype(BF)
                for b in (0, 1):
                    share_s[mine_too, b, hi, :, 256 * p:256 * p + 256] = value[T * b:T * b + T, :]
        if not mine_too:
            sib.start()
    sib.wait_recv()
    for b in (0, 1):
        for hi in (0, 1):
            value = share_s[1, b, hi].astype(F32) + sib_r[b, hi].astype(F32)
            pre_s[b, hi] = value.astype(BF)
    shares = []
    for n, (ctx, tp) in enumerate(me.group()):
        b = me.lo if n == 0 else 1 - me.lo
        hi = me.hi if n == 1 else 1 - me.hi
        shares.append(remote(pre_s.at[b, hi], share_r.at[me.lo, me.hi], share_ss.at[n], share_rs.at[n], (ctx, tp)))
        shares[n].start()
    share_r[me.lo, me.hi] = pre_s[me.lo, me.hi]

    dgated_x.all().wait_recv()
    for n in range(NB):
        b, pair = (n // 4) % 2, n - n % 8 + n % 4
        value = (dgated_r[pair, b].astype(F32) + dgated_r[pair + 4, b].astype(F32)).astype(BF).astype(F32)
        dlong = (value * short[0, n].astype(F32)).astype(BF)
        for g in range(G):
            row = 16 * (n // 2)
            D[g, row:row + 16, T * (n % 2):T * (n % 2) + T] = dlong[16 * g:16 * g + 16, :]
        dshort[0, n] = (value * longm[n].astype(F32)).astype(BF)

    def grad_of(streams, n):
        def step(r, c):
            for s in streams:
                x = dshort[s, pl.ds(BLK * r, BLK)].reshape(BLK * OWN, T)
                after = dshort[s, pl.ds(BLK * r + 1, BLK)].reshape(BLK * OWN, T)
                grad[pl.ds(BLK * r, BLK), s] = short_conv(s, x, after, SB, spread, BLK).astype(BF)
            return c

        lax.fori_loop(0, NB // BLK, step, 0)
        some = pl.ds(streams[0], len(streams))
        moved = Exchange(me, lambda to: grad.at[to, some], proj_grad.at[some, mine, :],
                         proj_grad.at[some, pl.ds(0, C - OWN), :], (x_ss.at[3 + n], x_rs.at[3 + n]))
        moved.start()
        own = pltpu.make_async_copy(grad.at[me.ctx, some], proj_grad.at[some, mine, :], local_s.at[7 + n])
        own.start()
        return moved, own

    grads = [grad_of((0,), 0)]
    conv_backward(D, M, skip_rows, dmix)

    def dkv_step(r, c):
        at_r = pl.ds(BLK * r, BLK)
        value = dmix[at_r].astype(F32)
        for s in (1, 2):
            dshort[s, at_r] = (value * short[3 - s, at_r].astype(F32)).astype(BF)
        return c

    lax.fori_loop(0, NB // BLK, dkv_step, 0)
    grads.append(grad_of((1, 2), 1))

    filter_gradient(X, D, XR, carry, gacc, filter_grad, SCALE)
    for c in shares:
        c.wait_recv()
    for b in (0, 1):
        for k in range(4):
            cols = slice(T * k, T * k + T)
            value = share_r[b, 0, :, cols].astype(F32) + share_r[b, 1, :, cols].astype(F32)
            block_out[512 * b + T * k:512 * b + T * k + T, :] = value.T.astype(BF)
    for c in relay.sends + cots + passes + [sib] + shares:
        c.wait_send()
    for x in (proj_x, gated_x, dgated_x):
        x.all().wait_send()
    for moved, own in grads:
        own.wait()
        moved.all().wait_send()
        moved.all().wait_recv()


def write_results(block_in, grad_in, filter_in, block_out, proj_grad, filter_grad, block, grad, filters, sems):
    pieces = [(grad_in.at[n], grad.at[n], proj_grad.at[n]) for n in range(3)]
    pieces += [(block_in, block, block_out), (filter_in, filters, filter_grad)]
    reads = [pltpu.make_async_copy(a, b, sems.at[0, n]) for n, (a, b, c) in enumerate(pieces)]
    writes = [pltpu.make_async_copy(b, c, sems.at[1, n]) for n, (a, b, c) in enumerate(pieces)]
    for c in reads:
        c.start()
    for r, c in zip(reads, writes):
        r.wait()
        c.start()
    for c in writes:
        c.wait()


def local(projected, conv_weight, filters, skip_gain, out_weight, cotangent):
    dma = pltpu.SemaphoreType.DMA
    vmem = pltpu.VMEM
    blocks = vmem((NB, OWN, T), BF)
    pairs = vmem((NB, 2, OWN, T), BF)
    shares = vmem((2, 2, T, 512), BF)
    scratch = dict(
        cw=vmem((3, TAPS, C), F32), filt=vmem((G, 4096), F32), skip=vmem((1, C), F32), taps=vmem((T, T), F32),
        spread=vmem((3 * TAPS + 1, OWN, T), F32), SF=vmem((2 * T, 6 * T), BF), SB=vmem((2 * T, 6 * T), BF),
        pr=vmem((NB + 1, 3, OWN, T), BF), pv=vmem((3, C, T), BF), wg=vmem((16, C, T), BF), cotg=vmem((2, 2048, T), BF),
        short=vmem((3, NB, OWN, T), BF), mix=blocks, longm=blocks, gated_s=vmem((16, 2, OWN, T), BF), gated_r=pairs,
        gated_t=vmem((2 * T, C), BF), acc=vmem((C, 2 * T), F32), dgated_s=pairs, dgated_r=pairs, dmix=blocks,
        dshort=vmem((3, NB + 1, OWN, T), BF), grad=vmem((NB, 3, OWN, T), BF), share_s=vmem((2, 2, 2, T, 512), BF),
        sib_r=shares, pre_s=shares, share_r=shares, hpad=vmem((G, 4096 + T), F32), M=vmem((G, 256, 4096 + T), BF),
        X=vmem((G, 512, 256), BF), D=vmem((G, 512, 256), BF), XR=vmem((G, 256, 256), BF), carry=vmem((G, T, T), F32),
        gacc=vmem((G, 4352), F32), local_s=dma((10,)),
        relay_ss=dma((40,)), relay_rs=dma((40,)), x_ss=dma((6,)), x_rs=dma((6,)), cot_ss=dma((3,)), cot_rs=dma((3,)),
        pass_ss=dma((4,)), pass_rs=dma((4,)), sib_ss=dma, sib_rs=dma, share_ss=dma((3,)), share_rs=dma((3,)))
    anywhere = pl.BlockSpec(memory_space=pl.ANY)
    whole = pl.BlockSpec(memory_space=pltpu.VMEM)
    block_out, proj_grad, filter_grad = pl.pallas_call(
        kernel,
        out_shape=(
            jax.ShapeDtypeStruct((C, T), BF),
            jax.ShapeDtypeStruct((3, C, T), BF),
            jax.ShapeDtypeStruct((G, 4096), F32),
        ),
        in_specs=[anywhere] * 6,
        out_specs=(whole, anywhere, whole),
        scratch_shapes=list(scratch.values()),
        compiler_params=pltpu.CompilerParams(collective_id=1, has_side_effects=True, vmem_limit_bytes=60 << 20),
        name="hyena_block",
    )(projected, conv_weight.transpose(1, 0, 2), filters[0], skip_gain[None], out_weight, cotangent)
    block_out, proj_grad, filter_grad = pl.pallas_call(
        write_results,
        out_shape=[jax.ShapeDtypeStruct(v.shape, v.dtype) for v in (block_out, proj_grad, filter_grad)],
        in_specs=[anywhere] * 3,
        out_specs=[anywhere] * 3,
        scratch_shapes=[vmem((C, T), BF), vmem((3, C, T), BF), vmem((G, 4096), F32), dma((2, 5))],
        name="write_results",
    )(block_out, proj_grad, filter_grad)
    return block_out, proj_grad, filter_grad[None]


def solution(mesh):
    return jax.shard_map(
        local,
        mesh=mesh,
        in_specs=(
            P(None, "tp", "ctx"),
            P(None, None, "tp"),
            P("tp", "ctx", None),
            P("tp"),
            P("tp", "ctx"),
            P("tp", "ctx"),
        ),
        out_specs=(P("tp", "ctx"), P(None, "tp", "ctx"), P("tp", "ctx", None)),
        check_vma=False,
    )
```
